32 devices in a mesh: inpair: 4 (over y, core), outpair: 8 (over z, x).
Axes of the slice: x: 2, y: 2, z: 4, core: 2. Of those that a mesh axis runs over, the one named last changes fastest.
Arguments:
- integrals: bfloat16 [4096, 8192], P('inpair', 'outpair'), may hold values from -0.09375 to 0.09375
- amplitudes: bfloat16 [8, 512, 4096], P('outpair', None, 'inpair'), may hold values from -6 to 6
- tile_live: int32 [16, 32], P('inpair', 'outpair'), may hold values 0 or 1
- batch_owner: int32 [2], replicated, may hold values from 0 to 7
- occ_energy: float32 [2, 512], P(None, 'inpair'), may hold values from -2 to -0.5
- vir_energy: float32 [8192], P('outpair'), may hold values from 0.5 to 4
- swap_within: int32 [128], replicated, may hold values from 0 to 127, each once
Outputs:
- update: float32 [2, 512, 8192], P(None, 'inpair', 'outpair')
The draws below stay inside these ranges and needn't reach their ends.
Inputs may be any that keep to these rules, and one draw needn't show every extreme that they name: `swap_within`: each value once.
All inputs are finite; a program needn't handle non-finite values. No bound on the sum of `tile_live` on one device may be relied on, other than what follows from the above.
Results may differ from the reference program's by a relative error of at most 0.0003.
Values may be sent and summed in bfloat16 or wider, within the bound.
No kernel may reach another device: no remote copies, remote signals or barrier semaphores. Data moves between devices by JAX's collectives and lax.ppermute only.
A program may use at most 64 MiB of HBM per device.

```python
import jax
import jax.numpy as jnp
from jax import lax

PAIR_IN = 1024
COLS_DEV = 1024
SUB_R = 256
SUB_C = 256
ROWS = 512
NB = 2
NCD = 4096
NAB = 8192
GRP = 128
N_INPAIR = 4
N_OUTPAIR = 8


def plant(values, key, smallest, high):
    shape = values.shape
    place = [jax.random.randint(jax.random.fold_in(key, axis), (), 0, shape[axis]) for axis in range(len(shape))]
    values = values.at[tuple(place)].set(smallest)
    longest = shape.index(max(shape))
    place[longest] = (place[longest] + 1) % shape[longest]
    return values.at[tuple(place)].set(high)


def with_spikes(array, stream_key, source, target, parts, factor):
    def block_of(axis_at):
        return (jnp.arange(array.shape[axis_at]) // (array.shape[axis_at] // parts)).reshape((-1,) + (1,) * (array.ndim - 1 - axis_at))

    first = jax.random.permutation(stream_key, parts)[block_of(target)]
    far = (block_of(target) + parts // 2) % parts
    return jnp.where((block_of(source) == first) | (block_of(source) == far), factor * array, array)


def block_levels(stream_key, shape, split, smallest, top_value):
    level = 1.0
    for dim, blocks in split:
        steps = jax.random.uniform(jax.random.fold_in(jax.random.fold_in(stream_key, 6), dim), (blocks,), jnp.float32, smallest / len(split), top_value / len(split))
        level = level * jnp.repeat(jnp.exp(steps), shape[dim] // blocks).reshape((-1,) + (1,) * (len(shape) - 1 - dim))
    return level


def centred(stream_key, dims, deviation, bound, split=(), held_as=jnp.bfloat16):
    loudness = block_levels(stream_key, dims, split, -0.22, 0.18) if split else 1.0
    values = jax.random.normal(stream_key, dims, jnp.float32) * deviation * loudness
    return jnp.minimum(jnp.maximum(values, -bound), bound).astype(held_as)


def heavy_noise(key, dims, spread, most, split, heavy, kind=jnp.bfloat16):
    result = spread * jax.random.normal(key, dims, jnp.float32)
    if split:
        result = result * block_levels(key, dims, split, -0.22, 0.18)
    return jnp.clip(with_spikes(result, jax.random.fold_in(key, 3), *heavy), -most, most).astype(kind)


def setup_inputs(seed: int = 0) -> dict:
    arg_keys = jax.random.split(jax.random.key(seed), 8)
    return {
        "integrals": centred(arg_keys[0], (NCD, NAB), NCD ** -0.5, 0.09375, ((0, 4), (1, 8))),
        "amplitudes": heavy_noise(arg_keys[1], (N_OUTPAIR, ROWS, NCD), 1.0, 6.0, ((0, 8), (2, 4)), (2, 1, 4, 2.0)),
        "tile_live": plant((jax.random.randint(arg_keys[2], (NCD // SUB_R, NAB // SUB_C), 0, 2) < 1).astype(jnp.int32), jax.random.fold_in(arg_keys[2], 1), 0, 1),
        "batch_owner": jax.random.randint(arg_keys[3], (NB,), 0, N_OUTPAIR).astype(jnp.int32),
        "occ_energy": jnp.clip(-2.0 + 1.5 * jax.random.uniform(arg_keys[4], (NB, ROWS), jnp.float32) ** block_levels(arg_keys[4], (NB, ROWS), ((1, 4),), -0.2, 0.2), -2.0, -0.5),
        "vir_energy": jnp.clip(0.5 + 3.5 * jax.random.uniform(arg_keys[5], (NAB,), jnp.float32) ** block_levels(arg_keys[5], (NAB,), ((0, 8),), -0.2, 0.2), 0.5, 4.0),
        "swap_within": jax.random.permutation(arg_keys[6], GRP).astype(jnp.int32),
    }


def reference(integrals, amplitudes, tile_live, batch_owner, occ_energy, vir_energy, swap_within):
    batch_rows = jnp.stack([amplitudes[batch_owner[index]] for index in range(NB)])
    batch_rows = batch_rows.reshape(NB * ROWS, PAIR_IN * N_INPAIR).astype(jnp.float32)
    count = N_OUTPAIR

    def column_block(block):
        columns = lax.dynamic_slice_in_dim(integrals, block * COLS_DEV, COLS_DEV, 1)
        flags = lax.dynamic_slice_in_dim(tile_live, block * (COLS_DEV // SUB_C), COLS_DEV // SUB_C, 1)
        tile_mask = jnp.repeat(jnp.repeat(flags, SUB_R, 0), SUB_C, 1).astype(jnp.bfloat16)
        weights = (columns * tile_mask).astype(jnp.float32)
        return jnp.dot(batch_rows, weights, preferred_element_type=jnp.float32, precision=lax.Precision.HIGHEST)

    blocks = lax.map(column_block, jnp.arange(count, dtype=jnp.int32))
    summed = jnp.transpose(blocks, (1, 0, 2)).reshape(NB, ROWS, COLS_DEV * N_OUTPAIR)
    pair_grid = summed.reshape(NB, ROWS, N_OUTPAIR, N_OUTPAIR, GRP)
    swapped = jnp.take(jnp.swapaxes(pair_grid, 2, 3), swap_within, axis=4).reshape(NB, ROWS, COLS_DEV * N_OUTPAIR)
    denominator = vir_energy[None, None, :] - occ_energy[:, :, None]
    return (summed + swapped) / denominator
```

```python
import functools

import jax
import jax.numpy as jnp
from jax import lax
from jax.experimental import pallas as pl
from jax.experimental.pallas import tpu as pltpu
from jax.sharding import PartitionSpec as P

CHUNKS = 4
PARTS = 2
LEVELS = 32767.0
OCTAVE = 128.0
LANES = 128
TILE_ROWS = 16
VMEM = 8 * 1024 * 1024


def pick(array, index, axis):
    return lax.dynamic_index_in_dim(array, index, axis, keepdims=False)


def tied(values, *others):
    return lax.optimization_barrier((values, *others))[0]


def codes_of(values):
    top = jnp.max(jnp.abs(values), axis=0, keepdims=True)
    code = jnp.ceil(jnp.log2(jnp.maximum(top, 1e-30)) * OCTAVE)
    scaled = jnp.round(values * (LEVELS * jnp.exp2(code * (-1.0 / OCTAVE))))
    return jnp.clip(scaled, -LEVELS, LEVELS), code


def step_of(code):
    return jnp.exp2(code.astype(jnp.float32) * (1.0 / OCTAVE)) * (1.0 / LEVELS)


def shrink(values):
    scaled, code = codes_of(values)
    return jnp.concatenate([scaled.astype(jnp.int16), code.astype(jnp.int16)], axis=0)


def grow(coded):
    return coded[:-1].astype(jnp.float32) * step_of(coded[-1:])


def merge_kernel(x_ref, keep_ref, coded_ref, total_ref, blocks_ref):
    x = x_ref[0]
    _, rows, _ = keep_ref.shape
    parties, _, lanes = blocks_ref.shape

    @pl.loop(0, parties)
    def _(o):
        at = pl.ds(pl.multiple_of(o * lanes, lanes), lanes)
        step = step_of(coded_ref[2 * rows : 2 * rows + 1, at].astype(jnp.int32))
        first = keep_ref[0, :, at] + coded_ref[:rows, at].astype(jnp.float32) * step
        second = keep_ref[1, :, at] + coded_ref[rows : 2 * rows, at].astype(jnp.float32) * step
        total = jnp.concatenate([jnp.where(x == 0, first, second), jnp.where(x == 0, second, first)], axis=0)
        total_ref[:, at] = total
        scaled, code = codes_of(total)
        blocks_ref[o, : 2 * rows] = scaled.astype(jnp.int32).astype(jnp.int16)
        blocks_ref[o, 2 * rows :] = jnp.broadcast_to(code, (TILE_ROWS, lanes)).astype(jnp.int32).astype(jnp.int16)


def merge(x, keep, coded, parties):
    _, rows, width = keep.shape
    lanes = width // parties
    if lanes % LANES or (2 * rows) % TILE_ROWS:
        total = keep + grow(coded).reshape(keep.shape)
        total = jnp.where(x == 0, total, total[::-1]).reshape(2 * rows, width)
        coded = shrink(total)
        return total, jnp.stack([coded[:, o * lanes : (o + 1) * lanes] for o in range(parties)])
    coded = jnp.concatenate([coded, jnp.zeros((TILE_ROWS - 1, width), jnp.int16)], axis=0)
    vmem = pl.BlockSpec(memory_space=pltpu.VMEM)
    return pl.pallas_call(
        merge_kernel,
        out_shape=(
            jax.ShapeDtypeStruct((2 * rows, width), jnp.float32),
            jax.ShapeDtypeStruct((parties, 2 * rows + TILE_ROWS, lanes), jnp.int16),
        ),
        in_specs=[pl.BlockSpec(memory_space=pltpu.SMEM), vmem, vmem],
        out_specs=(vmem, vmem),
        compiler_params=pltpu.CompilerParams(vmem_limit_bytes=VMEM),
        name="merge",
    )(x.reshape(1).astype(jnp.int32), keep, coded)


def finish_kernel(total_ref, blocks_ref, swap_ref, vir_ref, occ_ref, *rest):
    out_ref = rest[-1]
    parties, padded, lanes = blocks_ref.shape
    rows = padded - TILE_ROWS
    halves = rows // (out_ref.shape[0] * out_ref.shape[1])
    swap = jnp.broadcast_to(swap_ref[...], (rows, lanes))

    @pl.loop(0, parties)
    def _(o):
        at = pl.ds(pl.multiple_of(o * lanes, lanes), lanes)
        facing = blocks_ref[o, :rows].astype(jnp.float32) * step_of(blocks_ref[o, rows : rows + 1].astype(jnp.int32))
        both = total_ref[:, at] + jnp.take_along_axis(facing, swap, axis=1)
        both = both / (vir_ref[:, at] - occ_ref[...])
        both = both.reshape(2, -1, halves, lanes)
        for h in range(2):
            for b in range(both.shape[1]):
                out_ref[b, h, 0, :, at] = both[h, b]


def finish(total, blocks, swap_within, vir_energy, occ, out, part, parts):
    rows, width = total.shape
    parties, _, lanes = blocks.shape
    batches, share = occ.shape
    count = share // 2 // parts
    shape = (batches, 2, parts, count, width)
    occ = jnp.transpose(occ.reshape(batches, 2, parts, count)[:, :, part], (1, 0, 2)).reshape(rows, 1)
    whole = lambda a: pl.BlockSpec(a.shape, lambda i: (0,) * a.ndim)
    args = [total, blocks, swap_within.reshape(1, lanes), vir_energy.reshape(1, width), occ]
    specs = [whole(a) for a in args]
    alias = {}
    if out is not None:
        alias = {len(args): 0}
        args.append(out)
        specs.append(pl.BlockSpec(memory_space=pl.ANY))
    return pl.pallas_call(
        finish_kernel,
        grid=(1,),
        out_shape=jax.ShapeDtypeStruct(shape, jnp.float32),
        in_specs=specs,
        out_specs=pl.BlockSpec((batches, 2, 1, count, width), lambda i: (0, 0, part, 0, 0)),
        input_output_aliases=alias,
        compiler_params=pltpu.CompilerParams(vmem_limit_bytes=VMEM),
        name="finish",
    )(*args)


def on_device(integrals, amplitudes, tile_live, batch_owner, occ_energy, vir_energy, swap_within):
    parties, groups = lax.axis_size("outpair"), lax.axis_size("inpair")
    me, place = lax.axis_index("outpair"), lax.axis_index("inpair")
    x, z, nz = me % 2, me // 2, parties // 2
    batches = batch_owner.shape[0]
    _, rows, depth = amplitudes.shape
    width = integrals.shape[1]
    lanes = width // parties
    share = rows // groups
    half = share // 2
    parts, chunks = (PARTS, CHUNKS) if half % (16 * CHUNKS) == 0 else (1, 1)
    deep = half // chunks
    beside = [(o, o ^ 1) for o in range(parties)]
    even = [(o, o ^ 2) for o in range(parties) if (o ^ 2) < parties]
    odd = [(o, ((o // 2 + 1) ^ 1) * 2 - 2 + o % 2) for o in range(parties)]
    odd = [(o, t) for o, t in odd if 0 <= t < parties]

    stored = amplitudes[0].reshape(groups, 2, half, depth)
    mine = pick(stored, x, 1)
    other = pick(stored, 1 - x, 1)
    cut = lambda a, c: a[:, c * deep : (c + 1) * deep]
    tall_tile, wide_tile = integrals.shape[0] // tile_live.shape[0], width // tile_live.shape[1]
    flags = jnp.repeat(tile_live.astype(jnp.bfloat16), wide_tile, 1)[:, None, :]
    live = (integrals.reshape(-1, tall_tile, width) * flags).reshape(integrals.shape)

    home = [batch_owner[b] // 2 for b in range(batches)]
    column = [batch_owner[b] % 2 for b in range(batches)]
    from_even = [(z > home[b]) == (z % 2 == 1) for b in range(batches)]

    def swap_x(values):
        return lax.ppermute(values, "outpair", beside)

    def shift(values):
        return lax.ppermute(values, "outpair", odd), lax.ppermute(values, "outpair", even)

    source = []
    for c in range(chunks):
        came = swap_x(cut(other, c))
        source.append([jnp.where(column[b] == x, cut(mine, c), came) for b in range(batches)])

    held = []
    near, far = [], []
    moved = None
    for step in range(chunks + nz - 1):
        now = source[min(step, chunks - 1)]
        if step:
            ready = [far[c] for c in range(len(far)) if step - c - nz == 1]
            by_odd, by_even = tied(moved, *ready)
            now = [
                jnp.where(z == home[b], now[b], jnp.where(from_even[b], by_even[b], by_odd[b])) for b in range(batches)
            ]
        held.append(jnp.stack(now))
        if step < chunks + nz - 2:
            moved = shift(held[-1])
        if step >= nz - 1:
            window = held[step - nz + 1 : step + 1]
            got = [pick(jnp.stack([h[b] for h in window]), jnp.abs(z - home[b]), 0) for b in range(batches)]
            near.append(jnp.stack(got))
            far.append(swap_x(near[-1]))

    dot = lambda a, w: jnp.dot(a, w, preferred_element_type=jnp.float32)
    merged = []
    arrived = []
    for p in range(parts):
        mine = slice(p * chunks // parts, (p + 1) * chunks // parts)
        tall = jnp.stack([jnp.concatenate(near[mine], axis=2), jnp.concatenate(far[mine], axis=2)])
        if p:
            tall = tied(tall, merged[-1])
        count = tall.shape[3]
        tall = tall.reshape(2 * batches, groups // 2, 2, count, depth)
        away = pick(tall, 1 - place % 2, 2).reshape(-1, depth)
        stay = pick(tall, place % 2, 2).reshape(-1, depth)
        total = lax.ppermute(dot(away, live), "inpair", [(g, g ^ 1) for g in range(groups)])
        total = (dot(stay, live) + total).reshape(2 * batches, groups // 2, count, width)
        bit = 2
        while bit < groups:
            split = total.reshape(2 * batches, total.shape[1] // 2, 2, count, width)
            side = (place // bit) % 2
            keep, give = pick(split, side, 2), pick(split, 1 - side, 2)
            coded = lax.ppermute(shrink(give.reshape(-1, width)), "inpair", [(g, g ^ bit) for g in range(groups)])
            bit *= 2
            if bit < groups:
                total = keep + grow(coded).reshape(keep.shape)
        if p:
            coded = tied(coded, arrived[-1])
        total, blocks = merge(x, keep.reshape(2, batches * count, width), coded, parties)
        merged.append(total)
        arrived.append(lax.all_to_all(blocks, "outpair", split_axis=0, concat_axis=0, tiled=True))

    out = None
    parted = []
    for p in range(parts):
        total, blocks = merged[p], arrived[p]
        if lanes % LANES == 0:
            out = finish(total, blocks, swap_within, vir_energy, occ_energy, out, p, parts)
            continue
        facing = jnp.concatenate([jnp.take(grow(blocks[o]), swap_within, axis=1) for o in range(parties)], axis=1)
        parted.append((total + facing).reshape(2, batches, -1, width))
    if out is not None:
        return out.reshape(batches, share, width)
    whole = jnp.transpose(jnp.concatenate(parted, axis=2), (1, 0, 2, 3)).reshape(batches, share, width)
    return whole / (vir_energy[None, None, :] - occ_energy[:, :, None])


def solution(mesh):
    return jax.shard_map(
        on_device,
        mesh=mesh,
        in_specs=(
            P("inpair", "outpair"),
            P("outpair", None, "inpair"),
            P("inpair", "outpair"),
            P(),
            P(None, "inpair"),
            P("outpair"),
            P(),
        ),
        out_specs=P(None, "inpair", "outpair"),
        check_vma=False,
    )
```

```python
import jax
import jax.numpy as jnp
from jax import lax
from jax.experimental import pallas as pl
from jax.experimental.pallas import tpu as pltpu
from jax.sharding import PartitionSpec as P

CHUNKS = 4
PARTS = 2
LEVELS = 32767.0
OCTAVE = 128.0
LANES = 128
TILE_ROWS = 16
WIDE = 4
VMEM = 8 * 1024 * 1024
LONG = pl.CostEstimate(flops=20_000_000_000, bytes_accessed=0, transcendentals=0)


def pick(array, index, axis):
    return lax.dynamic_index_in_dim(array, index, axis, keepdims=False)


def tied(values, *others):
    return lax.optimization_barrier((values, *others))[0]


def codes_of(values):
    top = jnp.max(jnp.abs(values), axis=0, keepdims=True)
    code = jnp.ceil(jnp.log2(jnp.maximum(top, 1e-30)) * OCTAVE)
    scaled = jnp.round(values * (LEVELS * jnp.exp2(code * (-1.0 / OCTAVE))))
    return jnp.clip(scaled, -LEVELS, LEVELS), code


def step_of(code):
    return jnp.exp2(code.astype(jnp.float32) * (1.0 / OCTAVE)) * (1.0 / LEVELS)


def shrink(values):
    scaled, code = codes_of(values)
    return jnp.concatenate([scaled.astype(jnp.int16), code.astype(jnp.int16)], axis=0)


def grow(coded):
    return coded[:-1].astype(jnp.float32) * step_of(coded[-1:])


def times_kernel(a_ref, w_ref, out_ref):
    out_ref[...] = jnp.dot(a_ref[...], w_ref[...], preferred_element_type=jnp.float32)


def times(a, w, aligned):
    if not aligned:
        return jnp.dot(a, w, preferred_element_type=jnp.float32)
    vmem = pl.BlockSpec(memory_space=pltpu.VMEM)
    return pl.pallas_call(
        times_kernel,
        out_shape=jax.ShapeDtypeStruct((a.shape[0], w.shape[1]), jnp.float32),
        in_specs=[vmem, vmem],
        out_specs=vmem,
        cost_estimate=LONG,
        compiler_params=pltpu.CompilerParams(vmem_limit_bytes=VMEM),
        name="times",
    )(a, w)


def settle_kernel(side_ref, here_ref, there_ref, keep_ref, coded_ref):
    side = side_ref[0]
    parts, _, rows, width = here_ref.shape
    lanes = LANES

    for o in range(width // lanes):
        at = slice(o * lanes, (o + 1) * lanes)
        give = []
        for p in range(parts):
            pair = [here_ref[p, k, :, at] + there_ref[p, k, :, at] for k in range(2)]
            keep_ref[p * rows : (p + 1) * rows, at] = jnp.where(side == 0, pair[0], pair[1])
            give.append(jnp.where(side == 0, pair[1], pair[0]))
        scaled, code = codes_of(jnp.concatenate(give, axis=0))
        coded_ref[: parts * rows, at] = scaled.astype(jnp.int32).astype(jnp.int16)
        coded_ref[parts * rows :, at] = jnp.broadcast_to(code, (TILE_ROWS, lanes)).astype(jnp.int32).astype(jnp.int16)


def settle(side, here, there):
    parts, _, rows, width = here.shape
    vmem = pl.BlockSpec(memory_space=pltpu.VMEM)
    return pl.pallas_call(
        settle_kernel,
        out_shape=(
            jax.ShapeDtypeStruct((parts * rows, width), jnp.float32),
            jax.ShapeDtypeStruct((parts * rows + TILE_ROWS, width), jnp.int16),
        ),
        in_specs=[pl.BlockSpec(memory_space=pltpu.SMEM), vmem, vmem],
        out_specs=(vmem, vmem),
        compiler_params=pltpu.CompilerParams(vmem_limit_bytes=VMEM),
        name="settle",
    )(side, here, there)


def merge_kernel(left_ref, keep_ref, coded_ref, total_ref, blocks_ref):
    left = left_ref[0] == 1
    _, rows, _ = keep_ref.shape
    parties, _, lanes = blocks_ref.shape

    for o in range(parties):
        at = slice(o * lanes, (o + 1) * lanes)
        step = step_of(coded_ref[2 * rows : 2 * rows + 1, at].astype(jnp.int32))
        first = keep_ref[0, :, at] + coded_ref[:rows, at].astype(jnp.float32) * step
        second = keep_ref[1, :, at] + coded_ref[rows : 2 * rows, at].astype(jnp.float32) * step
        total = jnp.concatenate([jnp.where(left, first, second), jnp.where(left, second, first)], axis=0)
        total_ref[:, at] = total
        scaled, code = codes_of(total)
        blocks_ref[o, : 2 * rows] = scaled.astype(jnp.int32).astype(jnp.int16)
        blocks_ref[o, 2 * rows :] = jnp.broadcast_to(code, (TILE_ROWS, lanes)).astype(jnp.int32).astype(jnp.int16)


def merge(left, left_word, keep, coded, parties, aligned):
    _, rows, width = keep.shape
    lanes = width // parties
    if not aligned:
        total = keep + grow(coded).reshape(keep.shape)
        total = jnp.where(left, total, total[::-1]).reshape(2 * rows, width)
        coded = shrink(total)
        return total, jnp.stack([coded[:, o * lanes : (o + 1) * lanes] for o in range(parties)])
    vmem = pl.BlockSpec(memory_space=pltpu.VMEM)
    return pl.pallas_call(
        merge_kernel,
        out_shape=(
            jax.ShapeDtypeStruct((2 * rows, width), jnp.float32),
            jax.ShapeDtypeStruct((parties, 2 * rows + TILE_ROWS, lanes), jnp.int16),
        ),
        in_specs=[pl.BlockSpec(memory_space=pltpu.SMEM), vmem, vmem],
        out_specs=(vmem, vmem),
        cost_estimate=LONG,
        compiler_params=pltpu.CompilerParams(vmem_limit_bytes=VMEM),
        name="merge",
    )(left_word, keep, coded)


def finish_kernel(part, total_ref, blocks_ref, swap_ref, vir_ref, occ_ref, *rest):
    out_ref = rest[-1]
    batches, _, _, count, _ = out_ref.shape
    wide, padded, lanes = blocks_ref.shape
    rows = padded - TILE_ROWS
    half = occ_ref.shape[1] // 2
    swap = jnp.broadcast_to(swap_ref[...], (rows, lanes))
    occ = [jnp.transpose(jnp.broadcast_to(occ_ref[b : b + 1], (lanes, 2 * half))) for b in range(batches)]
    occ = [occ[b][h * half + part * count : h * half + (part + 1) * count] for h in range(2) for b in range(batches)]
    occ = jnp.concatenate(occ, axis=0)

    for o in range(wide):
        at = slice(o * lanes, (o + 1) * lanes)
        facing = blocks_ref[o, :rows].astype(jnp.float32) * step_of(blocks_ref[o, rows : rows + 1].astype(jnp.int32))
        both = total_ref[:, at] + jnp.take_along_axis(facing, swap, axis=1)
        both = both / (vir_ref[:, at] - occ)
        for h in range(2):
            for b in range(batches):
                first = (h * batches + b) * count
                out_ref[b, h, 0, :, at] = both[first : first + count]


def finish(total, blocks, swap_within, vir_energy, occ_energy, out, part, parts):
    rows, width = total.shape
    parties, padded, lanes = blocks.shape
    batches = occ_energy.shape[0]
    count = rows // 2 // batches
    wide = min(WIDE, parties)
    args = [total, blocks, swap_within.reshape(1, lanes), vir_energy.reshape(1, width), occ_energy]
    specs = [
        pl.BlockSpec((rows, wide * lanes), lambda i: (0, i)),
        pl.BlockSpec((wide, padded, lanes), lambda i: (i, 0, 0)),
        pl.BlockSpec((1, lanes), lambda i: (0, 0)),
        pl.BlockSpec((1, wide * lanes), lambda i: (0, i)),
        pl.BlockSpec(occ_energy.shape, lambda i: (0, 0)),
    ]
    alias = {}
    if out is not None:
        alias = {len(args): 0}
        args.append(out)
        specs.append(pl.BlockSpec(memory_space=pl.ANY))
    return pl.pallas_call(
        lambda *refs: finish_kernel(part, *refs),
        grid=(parties // wide,),
        out_shape=jax.ShapeDtypeStruct((batches, 2, parts, count, width), jnp.float32),
        in_specs=specs,
        out_specs=pl.BlockSpec((batches, 2, 1, count, wide * lanes), lambda i: (0, 0, part, 0, i)),
        input_output_aliases=alias,
        cost_estimate=LONG,
        compiler_params=pltpu.CompilerParams(vmem_limit_bytes=VMEM),
        name="finish",
    )(*args)


def on_device(integrals, amplitudes, tile_live, batch_owner, occ_energy, vir_energy, swap_within):
    parties, groups = lax.axis_size("outpair"), lax.axis_size("inpair")
    nz, bits = parties // 2, groups.bit_length() - 1
    batches = batch_owner.shape[0]
    _, rows, depth = amplitudes.shape
    width = integrals.shape[1]
    lanes = width // parties
    share = rows // groups
    half = share // 2
    parts, chunks = (PARTS, CHUNKS) if half % (16 * CHUNKS) == 0 else (1, 1)
    deep = half // chunks
    aligned = lanes % LANES == 0 and share % LANES == 0 and bits == 2
    beside = [(o, o ^ 1) for o in range(parties)]
    even = [(o, o ^ 2) for o in range(parties) if (o ^ 2) < parties]
    odd = [(o, ((o // 2 + 1) ^ 1) * 2 - 2 + o % 2) for o in range(parties)]
    odd = [(o, t) for o, t in odd if 0 <= t < parties]

    def swap_x(values):
        return lax.ppermute(values, "outpair", beside)

    def shift(values):
        return lax.ppermute(values, "outpair", odd), lax.ppermute(values, "outpair", even)

    def cut(a, c):
        return a[:, c * deep : (c + 1) * deep]

    me, place = lax.axis_index("outpair").astype(jnp.uint32), lax.axis_index("inpair").astype(jnp.uint32)
    x, z = me & 1, me >> 1
    stored = amplitudes[0].reshape(groups, 2, half, depth)
    other = pick(stored, 1 - x, 1)
    came = [swap_x(cut(other, c)) for c in range(chunks)]

    owner = [batch_owner[b].astype(jnp.uint32) for b in range(batches)]
    scalars = dict(
        x=x,
        left=x == 0,
        own=[z == o >> 1 for o in owner],
        mine=[x == o & 1 for o in owner],
        from_even=[(z > o >> 1) == (z & 1 == 1) for o in owner],
        far=[jnp.where(z > o >> 1, z - (o >> 1), (o >> 1) - z) for o in owner],
        side=[place >> k & 1 for k in range(bits)],
        not_side=[1 - (place >> k & 1) for k in range(bits)],
        left_word=(x == 0).astype(jnp.int32).reshape(1),
        side_word=(place >> 1 & 1).astype(jnp.int32).reshape(1),
    )
    tall_tile, wide_tile = integrals.shape[0] // tile_live.shape[0], width // tile_live.shape[1]
    flags = jnp.repeat(tile_live.astype(jnp.bfloat16), wide_tile, 1)[:, None, :]
    live = (integrals.reshape(-1, tall_tile, width) * flags).reshape(integrals.shape)
    mine = pick(stored, x, 1)
    came[0], live, mine, scalars = lax.optimization_barrier((came[0], live, mine, scalars))
    left, own, from_even, distance = scalars["left"], scalars["own"], scalars["from_even"], scalars["far"]
    side, not_side = scalars["side"], scalars["not_side"]

    source = [[jnp.where(m, cut(mine, c), came[c]) for m in scalars["mine"]] for c in range(chunks)]
    held, near, far = [], [], []
    keeps, sent, coded = {}, {}, {}

    def sum_part(p, n, f):
        tall = jnp.stack([jnp.concatenate(n, axis=2), jnp.concatenate(f, axis=2)])
        count = tall.shape[3]
        tall = tall.reshape(2 * batches, groups // 2, 2, count, depth)
        away = pick(tall, not_side[0], 2).reshape(-1, depth)
        stay = pick(tall, side[0], 2).reshape(-1, depth)
        there = lax.ppermute(times(away, live, aligned), "inpair", [(g, g ^ 1) for g in range(groups)])
        here = times(stay, live, aligned)
        across = lambda k: [(g, g ^ (1 << k)) for g in range(groups)]
        if aligned:
            shape = (2 * batches, 2, count, width)
            keep, sent[p] = settle(scalars["side_word"], here.reshape(shape), there.reshape(shape))
            coded[p] = lax.ppermute(sent[p], "inpair", across(1))
        else:
            total = (here + there).reshape(2 * batches, groups // 2, count, width)
            for k in range(1, bits):
                split = total.reshape(2 * batches, total.shape[1] // 2, 2, count, width)
                keep, give = pick(split, side[k], 2), pick(split, not_side[k], 2)
                sent[p] = shrink(give.reshape(-1, width))
                coded[p] = lax.ppermute(sent[p], "inpair", across(k))
                if k + 1 < bits:
                    total = keep + grow(coded[p]).reshape(keep.shape)
        keeps[p] = keep.reshape(2, batches * count, width)
        return sent[p]

    moved = None
    for step in range(chunks + nz - 1):
        now = source[min(step, chunks - 1)]
        if step:
            others = list(far[-1:])
            if parts > 1 and step == chunks + nz - 2:
                others.append(sum_part(0, near[: chunks // 2], far[: chunks // 2]))
            by_odd, by_even = tied(moved, *others)
            now = [
                jnp.where(own[b], now[b], jnp.where(from_even[b], by_even[b], by_odd[b])) for b in range(batches)
            ]
        held.append(jnp.stack(now))
        if step >= nz - 1:
            window = held[step - nz + 1 : step + 1]
            got = [pick(jnp.stack([h[b] for h in window]), distance[b], 0) for b in range(batches)]
            near.append(jnp.stack(got))
        if step >= nz - 1:
            far.append(swap_x(near[-1]))
        if step < chunks + nz - 2:
            moved = shift(tied(held[-1], *near[-1:]))

    word = scalars["left_word"]
    merged = {}
    if parts > 1:
        merged[0] = merge(left, word, keeps[0], coded[0], parties, aligned)
        n, f = tied((near[chunks // 2 :], far[chunks // 2 :]), merged[0])
    else:
        n, f = near, far
    sum_part(parts - 1, n, f)
    merged[parts - 1] = merge(left, word, keeps[parts - 1], coded[parts - 1], parties, aligned)
    order = range(parts)

    out, parted = None, []
    for p in order:
        total, blocks = merged[p]
        blocks = lax.all_to_all(blocks, "outpair", split_axis=0, concat_axis=0, tiled=True)
        if aligned:
            out = finish(total, blocks, swap_within, vir_energy, occ_energy, out, p, parts)
            continue
        facing = jnp.concatenate([jnp.take(grow(blocks[o]), swap_within, axis=1) for o in range(parties)], axis=1)
        parted.append((total + facing).reshape(2, batches, -1, width))
    if aligned:
        return out.reshape(batches, share, width)
    whole = jnp.transpose(jnp.concatenate(parted, axis=2), (1, 0, 2, 3)).reshape(batches, share, width)
    return whole / (vir_energy[None, None, :] - occ_energy[:, :, None])


def solution(mesh):
    return jax.shard_map(
        on_device,
        mesh=mesh,
        in_specs=(
            P("inpair", "outpair"),
            P("outpair", None, "inpair"),
            P("inpair", "outpair"),
            P(),
            P(None, "inpair"),
            P("outpair"),
            P(),
        ),
        out_specs=P(None, "inpair", "outpair"),
        check_vma=False,
    )
```

```python
import jax
import jax.numpy as jnp
from jax import lax
from jax.experimental import pallas as pl
from jax.experimental.pallas import tpu as pltpu
from jax.sharding import PartitionSpec as P

CHUNKS = 2
STREAMS = 2
LEVELS = 32767.0
OCTAVE = 128.0
LANES = 128
TILE_ROWS = 16
WIDE = 4
VMEM = 8 * 1024 * 1024
SHORT = pl.CostEstimate(flops=1_000_000, bytes_accessed=0, transcendentals=0)
LONG = pl.CostEstimate(flops=20_000_000_000, bytes_accessed=0, transcendentals=0)


def pick(array, index, axis):
    return lax.dynamic_index_in_dim(array, index, axis, keepdims=False)


def tied(values, *others):
    return lax.optimization_barrier((values, *others))[0]


def codes_of(values):
    top = jnp.max(jnp.abs(values), axis=0, keepdims=True)
    code = jnp.ceil(jnp.log2(jnp.maximum(top, 1e-30)) * OCTAVE)
    scaled = jnp.round(values * (LEVELS * jnp.exp2(code * (-1.0 / OCTAVE))))
    return jnp.clip(scaled, -LEVELS, LEVELS), code


def step_of(code):
    return jnp.exp2(code.astype(jnp.float32) * (1.0 / OCTAVE)) * (1.0 / LEVELS)


def shrink(values):
    scaled, code = codes_of(values)
    return jnp.concatenate([scaled.astype(jnp.int16), code.astype(jnp.int16)], axis=0)


def grow(coded):
    return coded[:-1].astype(jnp.float32) * step_of(coded[-1:])


def step_kernel(where_ref, mine_ref, came_ref, odd_ref, even_ref, out_ref):
    for b in range(out_ref.shape[0]):
        own, column, side = where_ref[b, 0] == 1, where_ref[b, 1] == 1, where_ref[b, 2] == 1

        @pl.when(own & column)
        def _():
            out_ref[b] = mine_ref[...]

        @pl.when(own & ~column)
        def _():
            out_ref[b] = came_ref[...]

        @pl.when(~own & side)
        def _():
            out_ref[b] = even_ref[b]

        @pl.when(~own & ~side)
        def _():
            out_ref[b] = odd_ref[b]


def step_on(where, mine, came, by_odd, by_even, cost):
    vmem = pl.BlockSpec(memory_space=pltpu.VMEM)
    return pl.pallas_call(
        step_kernel,
        out_shape=jax.ShapeDtypeStruct(by_odd.shape, by_odd.dtype),
        in_specs=[pl.BlockSpec(memory_space=pltpu.SMEM)] + [vmem] * 4,
        out_specs=vmem,
        cost_estimate=cost,
        compiler_params=pltpu.CompilerParams(vmem_limit_bytes=VMEM),
        name="step_on",
    )(where, mine, came, by_odd, by_even)


def flops(n):
    return pl.CostEstimate(flops=n, bytes_accessed=0, transcendentals=0)


def cost_of(step, q):
    return LONG if step < 4 or q == 1 else SHORT


def begin_kernel(where_ref, mine_ref, came_ref, out_ref):
    for b in range(out_ref.shape[0]):
        column = where_ref[b, 1] == 1

        @pl.when(column)
        def _():
            out_ref[b] = mine_ref[...]

        @pl.when(~column)
        def _():
            out_ref[b] = came_ref[...]


def begin(where, mine, came):
    vmem = pl.BlockSpec(memory_space=pltpu.VMEM)
    return pl.pallas_call(
        begin_kernel,
        out_shape=jax.ShapeDtypeStruct((where.shape[0], *mine.shape), mine.dtype),
        in_specs=[pl.BlockSpec(memory_space=pltpu.SMEM), vmem, vmem],
        out_specs=vmem,
        cost_estimate=LONG,
        compiler_params=pltpu.CompilerParams(vmem_limit_bytes=VMEM),
        name="begin",
    )(where, mine, came)


def choose_kernel(away_ref, *refs):
    out_ref = refs[-1]
    for b in range(out_ref.shape[0]):
        for k, ref in enumerate(refs[:-1]):

            @pl.when(away_ref[b] == k)
            def _():
                out_ref[b] = ref[b]


def choose(away, window):
    vmem = pl.BlockSpec(memory_space=pltpu.VMEM)
    return pl.pallas_call(
        choose_kernel,
        out_shape=jax.ShapeDtypeStruct(window[0].shape, window[0].dtype),
        in_specs=[pl.BlockSpec(memory_space=pltpu.SMEM)] + [vmem] * len(window),
        out_specs=vmem,
        cost_estimate=SHORT,
        compiler_params=pltpu.CompilerParams(vmem_limit_bytes=VMEM),
        name="choose",
    )(away, *window)


def times_kernel(a_ref, w_ref, out_ref):
    out_ref[...] = jnp.dot(a_ref[...], w_ref[...], preferred_element_type=jnp.float32)


def times(a, w, aligned, cost):
    if not aligned:
        return jnp.dot(a, w, preferred_element_type=jnp.float32)
    vmem = pl.BlockSpec(memory_space=pltpu.VMEM)
    return pl.pallas_call(
        times_kernel,
        out_shape=jax.ShapeDtypeStruct((a.shape[0], w.shape[1]), jnp.float32),
        in_specs=[vmem, vmem],
        out_specs=vmem,
        cost_estimate=cost,
        compiler_params=pltpu.CompilerParams(vmem_limit_bytes=VMEM),
        name="times",
    )(a, w)


def settle_kernel(side_ref, here_ref, there_ref, keep_ref, coded_ref):
    side = side_ref[0]
    parts, _, rows, width = here_ref.shape
    lanes = LANES

    for o in range(width // lanes):
        at = slice(o * lanes, (o + 1) * lanes)
        give = []
        for p in range(parts):
            pair = [here_ref[p, k, :, at] + there_ref[p, k, :, at] for k in range(2)]
            keep_ref[p * rows : (p + 1) * rows, at] = jnp.where(side == 0, pair[0], pair[1])
            give.append(jnp.where(side == 0, pair[1], pair[0]))
        scaled, code = codes_of(jnp.concatenate(give, axis=0))
        coded_ref[: parts * rows, at] = scaled.astype(jnp.int32).astype(jnp.int16)
        coded_ref[parts * rows :, at] = jnp.broadcast_to(code, (TILE_ROWS, lanes)).astype(jnp.int32).astype(jnp.int16)


def settle(side, here, there):
    parts, _, rows, width = here.shape
    vmem = pl.BlockSpec(memory_space=pltpu.VMEM)
    return pl.pallas_call(
        settle_kernel,
        out_shape=(
            jax.ShapeDtypeStruct((parts * rows, width), jnp.float32),
            jax.ShapeDtypeStruct((parts * rows + TILE_ROWS, width), jnp.int16),
        ),
        in_specs=[pl.BlockSpec(memory_space=pltpu.SMEM), vmem, vmem],
        out_specs=(vmem, vmem),
        compiler_params=pltpu.CompilerParams(vmem_limit_bytes=VMEM),
        name="settle",
    )(side, here, there)


def merge_kernel(left_ref, keep_ref, coded_ref, total_ref, blocks_ref):
    left = left_ref[0] == 1
    _, rows, _ = keep_ref.shape
    parties, _, lanes = blocks_ref.shape

    for o in range(parties):
        at = slice(o * lanes, (o + 1) * lanes)
        step = step_of(coded_ref[2 * rows : 2 * rows + 1, at].astype(jnp.int32))
        first = keep_ref[0, :, at] + coded_ref[:rows, at].astype(jnp.float32) * step
        second = keep_ref[1, :, at] + coded_ref[rows : 2 * rows, at].astype(jnp.float32) * step
        total = jnp.concatenate([jnp.where(left, first, second), jnp.where(left, second, first)], axis=0)
        total_ref[:, at] = total
        scaled, code = codes_of(total)
        blocks_ref[o, : 2 * rows] = scaled.astype(jnp.int32).astype(jnp.int16)
        blocks_ref[o, 2 * rows :] = jnp.broadcast_to(code, (TILE_ROWS, lanes)).astype(jnp.int32).astype(jnp.int16)


def merge(left, left_word, keep, coded, parties, aligned):
    _, rows, width = keep.shape
    lanes = width // parties
    if not aligned:
        total = keep + grow(coded).reshape(keep.shape)
        total = jnp.where(left, total, total[::-1]).reshape(2 * rows, width)
        coded = shrink(total)
        return total, jnp.stack([coded[:, o * lanes : (o + 1) * lanes] for o in range(parties)])
    vmem = pl.BlockSpec(memory_space=pltpu.VMEM)
    return pl.pallas_call(
        merge_kernel,
        out_shape=(
            jax.ShapeDtypeStruct((2 * rows, width), jnp.float32),
            jax.ShapeDtypeStruct((parties, 2 * rows + TILE_ROWS, lanes), jnp.int16),
        ),
        in_specs=[pl.BlockSpec(memory_space=pltpu.SMEM), vmem, vmem],
        out_specs=(vmem, vmem),
        cost_estimate=LONG,
        compiler_params=pltpu.CompilerParams(vmem_limit_bytes=VMEM),
        name="merge",
    )(left_word, keep, coded)


def finish_kernel(part, total_ref, blocks_ref, swap_ref, vir_ref, occ_ref, *rest):
    out_ref = rest[-1]
    batches, _, _, count, _ = out_ref.shape
    wide, padded, lanes = blocks_ref.shape
    rows = padded - TILE_ROWS
    half = occ_ref.shape[1] // 2
    swap = jnp.broadcast_to(swap_ref[...], (rows, lanes))
    occ = [jnp.transpose(jnp.broadcast_to(occ_ref[b : b + 1], (lanes, 2 * half))) for b in range(batches)]
    occ = [occ[b][h * half + part * count : h * half + (part + 1) * count] for h in range(2) for b in range(batches)]
    occ = jnp.concatenate(occ, axis=0)

    for o in range(wide):
        at = slice(o * lanes, (o + 1) * lanes)
        facing = blocks_ref[o, :rows].astype(jnp.float32) * step_of(blocks_ref[o, rows : rows + 1].astype(jnp.int32))
        both = total_ref[:, at] + jnp.take_along_axis(facing, swap, axis=1)
        both = both / (vir_ref[:, at] - occ)
        for h in range(2):
            for b in range(batches):
                first = (h * batches + b) * count
                out_ref[b, h, 0, :, at] = both[first : first + count]


def finish(total, blocks, swap_within, vir_energy, occ_energy, out, part, parts):
    rows, width = total.shape
    parties, padded, lanes = blocks.shape
    batches = occ_energy.shape[0]
    count = rows // 2 // batches
    wide = min(WIDE, parties)
    args = [total, blocks, swap_within.reshape(1, lanes), vir_energy.reshape(1, width), occ_energy]
    specs = [
        pl.BlockSpec((rows, wide * lanes), lambda i: (0, i)),
        pl.BlockSpec((wide, padded, lanes), lambda i: (i, 0, 0)),
        pl.BlockSpec((1, lanes), lambda i: (0, 0)),
        pl.BlockSpec((1, wide * lanes), lambda i: (0, i)),
        pl.BlockSpec(occ_energy.shape, lambda i: (0, 0)),
    ]
    alias = {}
    if out is not None:
        alias = {len(args): 0}
        args.append(out)
        specs.append(pl.BlockSpec(memory_space=pl.ANY))
    return pl.pallas_call(
        lambda *refs: finish_kernel(part, *refs),
        grid=(parties // wide,),
        out_shape=jax.ShapeDtypeStruct((batches, 2, parts, count, width), jnp.float32),
        in_specs=specs,
        out_specs=pl.BlockSpec((batches, 2, 1, count, wide * lanes), lambda i: (0, 0, part, 0, i)),
        input_output_aliases=alias,
        cost_estimate=LONG,
        compiler_params=pltpu.CompilerParams(vmem_limit_bytes=VMEM),
        name="finish",
    )(*args)


def on_device(integrals, amplitudes, tile_live, batch_owner, occ_energy, vir_energy, swap_within):
    parties, groups = lax.axis_size("outpair"), lax.axis_size("inpair")
    nz, bits = parties // 2, groups.bit_length() - 1
    batches = batch_owner.shape[0]
    _, rows, depth = amplitudes.shape
    width = integrals.shape[1]
    lanes = width // parties
    share = rows // groups
    half = share // 2
    streams, chunks = (STREAMS, CHUNKS) if half % (16 * STREAMS * CHUNKS) == 0 else (1, 1)
    parts = chunks
    deep = half // (streams * chunks)
    aligned = lanes % LANES == 0 and share % LANES == 0 and bits == 2
    beside = [(o, o ^ 1) for o in range(parties)]
    even = [(o, o ^ 2) for o in range(parties) if (o ^ 2) < parties]
    odd = [(o, ((o // 2 + 1) ^ 1) * 2 - 2 + o % 2) for o in range(parties)]
    odd = [(o, t) for o, t in odd if 0 <= t < parties]

    def swap_x(values):
        return lax.ppermute(values, "outpair", beside)

    def shift(values):
        return lax.ppermute(values, "outpair", odd), lax.ppermute(values, "outpair", even)

    def cut(a, q, c):
        return a[:, (c * streams + q) * deep : (c * streams + q + 1) * deep]

    me, place = lax.axis_index("outpair").astype(jnp.uint32), lax.axis_index("inpair").astype(jnp.uint32)
    x, z = me & 1, me >> 1
    stored = amplitudes[0].reshape(groups, 2, half, depth)
    other = pick(stored, 1 - x, 1)
    came = [[swap_x(cut(other, q, 0)) for q in range(streams)]]
    came += [swap_x(tied(jnp.stack([cut(other, q, c) for q in range(streams)]), came[0][0])) for c in range(1, chunks)]

    owner = [batch_owner[b].astype(jnp.uint32) for b in range(batches)]
    scalars = dict(
        x=x,
        left=x == 0,
        own=[z == o >> 1 for o in owner],
        mine=[x == o & 1 for o in owner],
        from_even=[(z > o >> 1) == (z & 1 == 1) for o in owner],
        far=[jnp.where(z > o >> 1, z - (o >> 1), (o >> 1) - z) for o in owner],
        side=[place >> k & 1 for k in range(bits)],
        not_side=[1 - (place >> k & 1) for k in range(bits)],
        where=jnp.stack(
            [
                jnp.stack([z == o >> 1, x == o & 1, (z > o >> 1) == (z & 1 == 1)]).astype(jnp.int32)
                for o in owner
            ]
        ),
        away=jnp.stack([jnp.where(z > o >> 1, z - (o >> 1), (o >> 1) - z).astype(jnp.int32) for o in owner]),
        left_word=(x == 0).astype(jnp.int32).reshape(1),
        side_word=(place >> 1 & 1).astype(jnp.int32).reshape(1),
    )
    tall_tile, wide_tile = integrals.shape[0] // tile_live.shape[0], width // tile_live.shape[1]
    flags = jnp.repeat(tile_live.astype(jnp.bfloat16), wide_tile, 1)[:, None, :]
    live = (integrals.reshape(-1, tall_tile, width) * flags).reshape(integrals.shape)
    mine = pick(stored, x, 1)
    came[0][0], live, mine, scalars = lax.optimization_barrier((came[0][0], live, mine, scalars))
    left, own, from_even, distance = scalars["left"], scalars["own"], scalars["from_even"], scalars["far"]
    side, not_side = scalars["side"], scalars["not_side"]

    keeps, sent, coded = {}, {}, {}

    def sum_part(p, n, f):
        tall = jnp.stack([jnp.concatenate(n, axis=2), jnp.concatenate(f, axis=2)])
        count = tall.shape[3]
        tall = tall.reshape(2 * batches, groups // 2, 2, count, depth)
        away = pick(tall, not_side[0], 2).reshape(-1, depth)
        stay = pick(tall, side[0], 2).reshape(-1, depth)
        there = lax.ppermute(times(away, live, aligned, LONG if p else SHORT), "inpair", [(g, g ^ 1) for g in range(groups)])
        here = times(stay, live, aligned, LONG if p else SHORT)
        across = lambda k: [(g, g ^ (1 << k)) for g in range(groups)]
        if aligned:
            shape = (2 * batches, 2, count, width)
            keep, sent[p] = settle(scalars["side_word"], here.reshape(shape), there.reshape(shape))
            coded[p] = lax.ppermute(sent[p], "inpair", across(1))
        else:
            total = (here + there).reshape(2 * batches, groups // 2, count, width)
            for k in range(1, bits):
                split = total.reshape(2 * batches, total.shape[1] // 2, 2, count, width)
                keep, give = pick(split, side[k], 2), pick(split, not_side[k], 2)
                sent[p] = shrink(give.reshape(-1, width))
                coded[p] = lax.ppermute(sent[p], "inpair", across(k))
                if k + 1 < bits:
                    total = keep + grow(coded[p]).reshape(keep.shape)
        keeps[p] = keep.reshape(2, batches * count, width)
        return sent[p]

    def advance(q, c, by_odd, by_even, cost):
        if aligned:
            return step_on(scalars["where"], cut(mine, q, c), came[c][q], by_odd, by_even, cost)
        own_chunk = [jnp.where(m, cut(mine, q, c), came[c][q]) for m in scalars["mine"]]
        return jnp.stack(
            [jnp.where(own[b], own_chunk[b], jnp.where(from_even[b], by_even[b], by_odd[b])) for b in range(batches)]
        )

    def settled(window):
        if aligned:
            return choose(scalars["away"], window)
        return jnp.stack([pick(jnp.stack([h[b] for h in window]), distance[b], 0) for b in range(batches)])

    held = []
    near, far = [[] for _ in range(streams)], [[] for _ in range(streams)]
    for q in range(streams):
        if aligned:
            start = begin(scalars["where"], cut(mine, q, 0), came[0][q])
        else:
            start = jnp.stack([jnp.where(m, cut(mine, q, 0), came[0][q]) for m in scalars["mine"]])
        held.append([start])
    moved = [shift(h[0]) for h in held]
    for step in range(1, chunks + nz - 1):
        for q in range(streams):
            arrived = moved[q]
            held[q].append(advance(q, min(step, chunks - 1), *arrived, cost_of(step, q)))
            if step < chunks + nz - 2:
                moved[q] = shift(held[q][-1])
            if step >= nz - 1:
                near[q].append(settled(held[q][step - nz + 1 : step + 1]))
                far[q].append(swap_x(near[q][-1]))

    word = scalars["left_word"]
    merged = {}
    for p in range(parts):
        n, f = [near[q][p] for q in range(streams)], [far[q][p] for q in range(streams)]
        if p:
            n, f = tied((n, f), *[sent[k] for k in range(p)])
        sum_part(p, n, f)
    for p in range(parts):
        back = tied(coded[p], *[sent[k] for k in range(p + 1, parts)])
        merged[p] = merge(left, word, keeps[p], back, parties, aligned)
    order = range(parts)

    out, parted = None, []
    for p in order:
        total, blocks = merged[p]
        blocks = lax.all_to_all(blocks, "outpair", split_axis=0, concat_axis=0, tiled=True)
        if aligned:
            out = finish(total, blocks, swap_within, vir_energy, occ_energy, out, p, parts)
            continue
        facing = jnp.concatenate([jnp.take(grow(blocks[o]), swap_within, axis=1) for o in range(parties)], axis=1)
        parted.append((total + facing).reshape(2, batches, -1, width))
    if aligned:
        return out.reshape(batches, share, width)
    whole = jnp.transpose(jnp.concatenate(parted, axis=2), (1, 0, 2, 3)).reshape(batches, share, width)
    return whole / (vir_energy[None, None, :] - occ_energy[:, :, None])


def solution(mesh):
    return jax.shard_map(
        on_device,
        mesh=mesh,
        in_specs=(
            P("inpair", "outpair"),
            P("outpair", None, "inpair"),
            P("inpair", "outpair"),
            P(),
            P(None, "inpair"),
            P("outpair"),
            P(),
        ),
        out_specs=P(None, "inpair", "outpair"),
        check_vma=False,
    )
```

```python
import jax
import jax.numpy as jnp
from jax import lax
from jax.experimental import pallas as pl
from jax.experimental.pallas import tpu as pltpu
from jax.sharding import PartitionSpec as P

CHUNKS = 2
STREAMS = 2
LEVELS = 32767.0
OCTAVE = 128.0
LANES = 128
TILE_ROWS = 16
WIDE = 4
VMEM = 8 * 1024 * 1024
SHORT = pl.CostEstimate(flops=1_000_000, bytes_accessed=0, transcendentals=0)
LONG = pl.CostEstimate(flops=20_000_000_000, bytes_accessed=0, transcendentals=0)


def pick(array, index, axis):
    return lax.dynamic_index_in_dim(array, index, axis, keepdims=False)


def tied(values, *others):
    return lax.optimization_barrier((values, *others))[0]


def codes_of(values):
    top = jnp.max(jnp.abs(values), axis=0, keepdims=True)
    code = jnp.ceil(jnp.log2(jnp.maximum(top, 1e-30)) * OCTAVE)
    scaled = jnp.round(values * (LEVELS * jnp.exp2(code * (-1.0 / OCTAVE))))
    return jnp.clip(scaled, -LEVELS, LEVELS), code


def step_of(code):
    return jnp.exp2(code.astype(jnp.float32) * (1.0 / OCTAVE)) * (1.0 / LEVELS)


def shrink(values):
    scaled, code = codes_of(values)
    return jnp.concatenate([scaled.astype(jnp.int16), code.astype(jnp.int16)], axis=0)


def grow(coded):
    return coded[:-1].astype(jnp.float32) * step_of(coded[-1:])


def step_kernel(*refs):
    mine_ref, came_ref, odd_ref, even_ref, out_ref = refs[-5:]
    for b in range(out_ref.shape[0]):
        own, column, side = [refs[b][0] >> k & 1 == 1 for k in range(3)]

        @pl.when(own & column)
        def _():
            out_ref[b] = mine_ref[...]

        @pl.when(own & ~column)
        def _():
            out_ref[b] = came_ref[...]

        @pl.when(~own & side)
        def _():
            out_ref[b] = even_ref[b]

        @pl.when(~own & ~side)
        def _():
            out_ref[b] = odd_ref[b]


def step_on(words, mine, came, by_odd, by_even, cost):
    vmem = pl.BlockSpec(memory_space=pltpu.VMEM)
    return pl.pallas_call(
        step_kernel,
        out_shape=jax.ShapeDtypeStruct(by_odd.shape, by_odd.dtype),
        in_specs=[pl.BlockSpec(memory_space=pltpu.SMEM)] * len(words) + [vmem] * 4,
        out_specs=vmem,
        cost_estimate=cost,
        compiler_params=pltpu.CompilerParams(vmem_limit_bytes=VMEM),
        name="step_on",
    )(*words, mine, came, by_odd, by_even)


def flops(n):
    return pl.CostEstimate(flops=n, bytes_accessed=0, transcendentals=0)


def cost_of(step, q):
    return LONG if step < 4 or q == 1 else SHORT


def begin_kernel(*refs):
    mine_ref, came_ref, out_ref = refs[-3:]
    for b in range(out_ref.shape[0]):
        column = refs[b][0] >> 1 & 1 == 1

        @pl.when(column)
        def _():
            out_ref[b] = mine_ref[...]

        @pl.when(~column)
        def _():
            out_ref[b] = came_ref[...]


def begin(words, mine, came):
    vmem = pl.BlockSpec(memory_space=pltpu.VMEM)
    return pl.pallas_call(
        begin_kernel,
        out_shape=jax.ShapeDtypeStruct((len(words), *mine.shape), mine.dtype),
        in_specs=[pl.BlockSpec(memory_space=pltpu.SMEM)] * len(words) + [vmem] * 2,
        out_specs=vmem,
        cost_estimate=LONG,
        compiler_params=pltpu.CompilerParams(vmem_limit_bytes=VMEM),
        name="begin",
    )(*words, mine, came)


def choose_kernel(*refs):
    out_ref = refs[-1]
    batches = out_ref.shape[0]
    for b in range(batches):
        for k, ref in enumerate(refs[batches:-1]):

            @pl.when(refs[b][0] >> 3 == k)
            def _():
                out_ref[b] = ref[b]


def choose(words, window):
    vmem = pl.BlockSpec(memory_space=pltpu.VMEM)
    return pl.pallas_call(
        choose_kernel,
        out_shape=jax.ShapeDtypeStruct(window[0].shape, window[0].dtype),
        in_specs=[pl.BlockSpec(memory_space=pltpu.SMEM)] * len(words) + [vmem] * len(window),
        out_specs=vmem,
        cost_estimate=SHORT,
        compiler_params=pltpu.CompilerParams(vmem_limit_bytes=VMEM),
        name="choose",
    )(*words, *window)


def times_kernel(a_ref, w_ref, out_ref):
    out_ref[...] = jnp.dot(a_ref[...], w_ref[...], preferred_element_type=jnp.float32)


def times(a, w, aligned, cost):
    if not aligned:
        return jnp.dot(a, w, preferred_element_type=jnp.float32)
    vmem = pl.BlockSpec(memory_space=pltpu.VMEM)
    return pl.pallas_call(
        times_kernel,
        out_shape=jax.ShapeDtypeStruct((a.shape[0], w.shape[1]), jnp.float32),
        in_specs=[vmem, vmem],
        out_specs=vmem,
        cost_estimate=cost,
        compiler_params=pltpu.CompilerParams(vmem_limit_bytes=VMEM),
        name="times",
    )(a, w)


def settle_kernel(side_ref, here_ref, there_ref, keep_ref, coded_ref):
    side = side_ref[0]
    parts, _, rows, width = here_ref.shape
    lanes = LANES

    for o in range(width // lanes):
        at = slice(o * lanes, (o + 1) * lanes)
        give = []
        for p in range(parts):
            pair = [here_ref[p, k, :, at] + there_ref[p, k, :, at] for k in range(2)]
            keep_ref[p * rows : (p + 1) * rows, at] = jnp.where(side == 0, pair[0], pair[1])
            give.append(jnp.where(side == 0, pair[1], pair[0]))
        scaled, code = codes_of(jnp.concatenate(give, axis=0))
        coded_ref[: parts * rows, at] = scaled.astype(jnp.int32).astype(jnp.int16)
        coded_ref[parts * rows :, at] = jnp.broadcast_to(code, (TILE_ROWS, lanes)).astype(jnp.int32).astype(jnp.int16)


def settle(side, here, there):
    parts, _, rows, width = here.shape
    vmem = pl.BlockSpec(memory_space=pltpu.VMEM)
    return pl.pallas_call(
        settle_kernel,
        out_shape=(
            jax.ShapeDtypeStruct((parts * rows, width), jnp.float32),
            jax.ShapeDtypeStruct((parts * rows + TILE_ROWS, width), jnp.int16),
        ),
        in_specs=[pl.BlockSpec(memory_space=pltpu.SMEM), vmem, vmem],
        out_specs=(vmem, vmem),
        compiler_params=pltpu.CompilerParams(vmem_limit_bytes=VMEM),
        name="settle",
    )(side, here, there)


def merge_kernel(left_ref, keep_ref, coded_ref, total_ref, blocks_ref):
    left = left_ref[0] == 1
    _, rows, _ = keep_ref.shape
    parties, _, lanes = blocks_ref.shape

    for o in range(parties):
        at = slice(o * lanes, (o + 1) * lanes)
        step = step_of(coded_ref[2 * rows : 2 * rows + 1, at].astype(jnp.int32))
        first = keep_ref[0, :, at] + coded_ref[:rows, at].astype(jnp.float32) * step
        second = keep_ref[1, :, at] + coded_ref[rows : 2 * rows, at].astype(jnp.float32) * step
        total = jnp.concatenate([jnp.where(left, first, second), jnp.where(left, second, first)], axis=0)
        total_ref[:, at] = total
        scaled, code = codes_of(total)
        blocks_ref[o, : 2 * rows] = scaled.astype(jnp.int32).astype(jnp.int16)
        blocks_ref[o, 2 * rows :] = jnp.broadcast_to(code, (TILE_ROWS, lanes)).astype(jnp.int32).astype(jnp.int16)


def merge(left, left_word, keep, coded, parties, aligned):
    _, rows, width = keep.shape
    lanes = width // parties
    if not aligned:
        total = keep + grow(coded).reshape(keep.shape)
        total = jnp.where(left, total, total[::-1]).reshape(2 * rows, width)
        coded = shrink(total)
        return total, jnp.stack([coded[:, o * lanes : (o + 1) * lanes] for o in range(parties)])
    vmem = pl.BlockSpec(memory_space=pltpu.VMEM)
    return pl.pallas_call(
        merge_kernel,
        out_shape=(
            jax.ShapeDtypeStruct((2 * rows, width), jnp.float32),
            jax.ShapeDtypeStruct((parties, 2 * rows + TILE_ROWS, lanes), jnp.int16),
        ),
        in_specs=[pl.BlockSpec(memory_space=pltpu.SMEM), vmem, vmem],
        out_specs=(vmem, vmem),
        cost_estimate=SHORT,
        compiler_params=pltpu.CompilerParams(vmem_limit_bytes=VMEM),
        name="merge",
    )(left_word, keep, coded)


def finish_kernel(part, total_ref, blocks_ref, swap_ref, vir_ref, occ_ref, *rest):
    out_ref = rest[-1]
    batches, _, _, count, _ = out_ref.shape
    wide, padded, lanes = blocks_ref.shape
    rows = padded - TILE_ROWS
    half = occ_ref.shape[1] // 2
    swap = jnp.broadcast_to(swap_ref[...], (rows, lanes))
    occ = [jnp.transpose(jnp.broadcast_to(occ_ref[b : b + 1], (lanes, 2 * half))) for b in range(batches)]
    occ = [occ[b][h * half + part * count : h * half + (part + 1) * count] for h in range(2) for b in range(batches)]
    occ = jnp.concatenate(occ, axis=0)

    for o in range(wide):
        at = slice(o * lanes, (o + 1) * lanes)
        facing = blocks_ref[o, :rows].astype(jnp.float32) * step_of(blocks_ref[o, rows : rows + 1].astype(jnp.int32))
        both = total_ref[:, at] + jnp.take_along_axis(facing, swap, axis=1)
        both = both / (vir_ref[:, at] - occ)
        for h in range(2):
            for b in range(batches):
                first = (h * batches + b) * count
                out_ref[b, h, 0, :, at] = both[first : first + count]


def finish(total, blocks, swap_within, vir_energy, occ_energy, out, part, parts):
    rows, width = total.shape
    parties, padded, lanes = blocks.shape
    batches = occ_energy.shape[0]
    count = rows // 2 // batches
    wide = min(WIDE, parties)
    args = [total, blocks, swap_within.reshape(1, lanes), vir_energy.reshape(1, width), occ_energy]
    specs = [
        pl.BlockSpec((rows, wide * lanes), lambda i: (0, i)),
        pl.BlockSpec((wide, padded, lanes), lambda i: (i, 0, 0)),
        pl.BlockSpec((1, lanes), lambda i: (0, 0)),
        pl.BlockSpec((1, wide * lanes), lambda i: (0, i)),
        pl.BlockSpec(occ_energy.shape, lambda i: (0, 0)),
    ]
    alias = {}
    if out is not None:
        alias = {len(args): 0}
        args.append(out)
        specs.append(pl.BlockSpec(memory_space=pl.ANY))
    return pl.pallas_call(
        lambda *refs: finish_kernel(part, *refs),
        grid=(parties // wide,),
        out_shape=jax.ShapeDtypeStruct((batches, 2, parts, count, width), jnp.float32),
        in_specs=specs,
        out_specs=pl.BlockSpec((batches, 2, 1, count, wide * lanes), lambda i: (0, 0, part, 0, i)),
        input_output_aliases=alias,
        cost_estimate=LONG,
        compiler_params=pltpu.CompilerParams(vmem_limit_bytes=VMEM),
        name="finish",
    )(*args)


def on_device(integrals, amplitudes, tile_live, batch_owner, occ_energy, vir_energy, swap_within):
    parties, groups = lax.axis_size("outpair"), lax.axis_size("inpair")
    nz, bits = parties // 2, groups.bit_length() - 1
    batches = batch_owner.shape[0]
    _, rows, depth = amplitudes.shape
    width = integrals.shape[1]
    lanes = width // parties
    share = rows // groups
    half = share // 2
    streams, chunks = (STREAMS, CHUNKS) if half % (16 * STREAMS * CHUNKS) == 0 else (1, 1)
    parts = chunks
    deep = half // (streams * chunks)
    aligned = lanes % LANES == 0 and share % LANES == 0 and bits == 2
    beside = [(o, o ^ 1) for o in range(parties)]
    even = [(o, o ^ 2) for o in range(parties) if (o ^ 2) < parties]
    odd = [(o, ((o // 2 + 1) ^ 1) * 2 - 2 + o % 2) for o in range(parties)]
    odd = [(o, t) for o, t in odd if 0 <= t < parties]

    def swap_x(values):
        return lax.ppermute(values, "outpair", beside)

    def shift(values):
        return lax.ppermute(values, "outpair", odd), lax.ppermute(values, "outpair", even)

    def cut(a, q, c):
        return a[:, (c * streams + q) * deep : (c * streams + q + 1) * deep]

    me, place = lax.axis_index("outpair").astype(jnp.uint32), lax.axis_index("inpair").astype(jnp.uint32)
    x, z = me & 1, me >> 1
    stored = amplitudes[0].reshape(groups, 2, half, depth)
    other = pick(stored, 1 - x, 1)
    came = [[swap_x(cut(other, 0, 0))]]
    came[0] += [swap_x(tied(cut(other, q, 0), came[0][0])) for q in range(1, streams)]
    came += [swap_x(tied(jnp.stack([cut(other, q, c) for q in range(streams)]), came[0][0])) for c in range(1, chunks)]

    owner = [batch_owner[b].astype(jnp.uint32) for b in range(batches)]
    scalars = dict(
        x=x,
        left=x == 0,
        own=[z == o >> 1 for o in owner],
        mine=[x == o & 1 for o in owner],
        from_even=[(z > o >> 1) == (z & 1 == 1) for o in owner],
        far=[jnp.where(z > o >> 1, z - (o >> 1), (o >> 1) - z) for o in owner],
        side=[place >> k & 1 for k in range(bits)],
        not_side=[1 - (place >> k & 1) for k in range(bits)],
        words=[
            (
                (z == o >> 1).astype(jnp.int32)
                + 2 * (x == o & 1).astype(jnp.int32)
                + 4 * ((z > o >> 1) == (z & 1 == 1)).astype(jnp.int32)
                + 8 * jnp.where(z > o >> 1, z - (o >> 1), (o >> 1) - z).astype(jnp.int32)
            ).reshape(1)
            for o in owner
        ],
        left_word=(x == 0).astype(jnp.int32).reshape(1),
        side_word=(place >> 1 & 1).astype(jnp.int32).reshape(1),
    )
    tall_tile, wide_tile = integrals.shape[0] // tile_live.shape[0], width // tile_live.shape[1]
    flags = jnp.repeat(tile_live.astype(jnp.bfloat16), wide_tile, 1)[:, None, :]
    live = (integrals.reshape(-1, tall_tile, width) * flags).reshape(integrals.shape)
    mine = pick(stored, x, 1)
    came[0][0], live, mine, scalars = lax.optimization_barrier((came[0][0], live, mine, scalars))
    left, own, from_even, distance = scalars["left"], scalars["own"], scalars["from_even"], scalars["far"]
    side, not_side = scalars["side"], scalars["not_side"]

    keeps, sent, coded = {}, {}, {}

    def sum_part(p, n, f):
        tall = jnp.stack([jnp.concatenate(n, axis=2), jnp.concatenate(f, axis=2)])
        count = tall.shape[3]
        tall = tall.reshape(2 * batches, groups // 2, 2, count, depth)
        away = pick(tall, not_side[0], 2).reshape(-1, depth)
        stay = pick(tall, side[0], 2).reshape(-1, depth)
        there = lax.ppermute(times(away, live, aligned, LONG if p else SHORT), "inpair", [(g, g ^ 1) for g in range(groups)])
        here = times(stay, live, aligned, LONG if p else SHORT)
        across = lambda k: [(g, g ^ (1 << k)) for g in range(groups)]
        if aligned:
            shape = (2 * batches, 2, count, width)
            keep, sent[p] = settle(scalars["side_word"], here.reshape(shape), there.reshape(shape))
            coded[p] = lax.ppermute(sent[p], "inpair", across(1))
        else:
            total = (here + there).reshape(2 * batches, groups // 2, count, width)
            for k in range(1, bits):
                split = total.reshape(2 * batches, total.shape[1] // 2, 2, count, width)
                keep, give = pick(split, side[k], 2), pick(split, not_side[k], 2)
                sent[p] = shrink(give.reshape(-1, width))
                coded[p] = lax.ppermute(sent[p], "inpair", across(k))
                if k + 1 < bits:
                    total = keep + grow(coded[p]).reshape(keep.shape)
        keeps[p] = keep.reshape(2, batches * count, width)
        return sent[p]

    def advance(q, c, by_odd, by_even, cost):
        if aligned:
            return step_on(scalars["words"], cut(mine, q, c), came[c][q], by_odd, by_even, cost)
        own_chunk = [jnp.where(m, cut(mine, q, c), came[c][q]) for m in scalars["mine"]]
        return jnp.stack(
            [jnp.where(own[b], own_chunk[b], jnp.where(from_even[b], by_even[b], by_odd[b])) for b in range(batches)]
        )

    def settled(window):
        if aligned:
            return choose(scalars["words"], window)
        return jnp.stack([pick(jnp.stack([h[b] for h in window]), distance[b], 0) for b in range(batches)])

    held = []
    near, far = [[] for _ in range(streams)], [[] for _ in range(streams)]
    for q in range(streams):
        if aligned:
            start = begin(scalars["words"], cut(mine, q, 0), came[0][q])
        else:
            start = jnp.stack([jnp.where(m, cut(mine, q, 0), came[0][q]) for m in scalars["mine"]])
        held.append([start])
    moved = [shift(h[0]) for h in held]
    for step in range(1, chunks + nz - 1):
        for q in range(streams):
            arrived = moved[q]
            held[q].append(advance(q, min(step, chunks - 1), *arrived, cost_of(step, q)))
            if step < chunks + nz - 2:
                moved[q] = shift(held[q][-1])
            if step >= nz - 1:
                near[q].append(settled(held[q][step - nz + 1 : step + 1]))
                far[q].append(swap_x(near[q][-1]))

    word = scalars["left_word"]
    merged = {}
    for p in range(parts):
        n, f = [near[q][p] for q in range(streams)], [far[q][p] for q in range(streams)]
        if p:
            n, f = tied((n, f), *[sent[k] for k in range(p)])
        sum_part(p, n, f)
    for p in range(parts):
        back = tied(coded[p], *[sent[k] for k in range(p + 1, parts)])
        merged[p] = merge(left, word, keeps[p], back, parties, aligned)
    order = range(parts)

    out, parted = None, []
    for p in order:
        total, blocks = merged[p]
        blocks = lax.all_to_all(blocks, "outpair", split_axis=0, concat_axis=0, tiled=True)
        if aligned:
            out = finish(total, blocks, swap_within, vir_energy, occ_energy, out, p, parts)
            continue
        facing = jnp.concatenate([jnp.take(grow(blocks[o]), swap_within, axis=1) for o in range(parties)], axis=1)
        parted.append((total + facing).reshape(2, batches, -1, width))
    if aligned:
        return out.reshape(batches, share, width)
    whole = jnp.transpose(jnp.concatenate(parted, axis=2), (1, 0, 2, 3)).reshape(batches, share, width)
    return whole / (vir_energy[None, None, :] - occ_energy[:, :, None])


def solution(mesh):
    return jax.shard_map(
        on_device,
        mesh=mesh,
        in_specs=(
            P("inpair", "outpair"),
            P("outpair", None, "inpair"),
            P("inpair", "outpair"),
            P(),
            P(None, "inpair"),
            P("outpair"),
            P(),
        ),
        out_specs=P(None, "inpair", "outpair"),
        check_vma=False,
    )
```

```python
import jax
import jax.numpy as jnp
from jax import lax
from jax.experimental import pallas as pl
from jax.experimental.pallas import tpu as pltpu
from jax.sharding import PartitionSpec as P

CHUNKS = 2
STREAMS = 2
LEVELS = 32767.0
OCTAVE = 128.0
LANES = 128
TILE_ROWS = 16
WIDE = 4
VMEM = 8 * 1024 * 1024
SHORT = pl.CostEstimate(flops=1_000_000, bytes_accessed=0, transcendentals=0)
LONG = pl.CostEstimate(flops=20_000_000_000, bytes_accessed=0, transcendentals=0)


def pick(array, index, axis):
    return lax.dynamic_index_in_dim(array, index, axis, keepdims=False)


def tied(values, *others):
    return lax.optimization_barrier((values, *others))[0]


def codes_of(values):
    top = jnp.max(jnp.abs(values), axis=0, keepdims=True)
    code = jnp.ceil(jnp.log2(jnp.maximum(top, 1e-30)) * OCTAVE)
    scaled = jnp.round(values * (LEVELS * jnp.exp2(code * (-1.0 / OCTAVE))))
    return jnp.clip(scaled, -LEVELS, LEVELS), code


def step_of(code):
    return jnp.exp2(code.astype(jnp.float32) * (1.0 / OCTAVE)) * (1.0 / LEVELS)


def shrink(values):
    scaled, code = codes_of(values)
    return jnp.concatenate([scaled.astype(jnp.int16), code.astype(jnp.int16)], axis=0)


def grow(coded):
    return coded[:-1].astype(jnp.float32) * step_of(coded[-1:])


def step_kernel(*refs):
    mine_ref, came_ref, odd_ref, even_ref, out_ref = refs[-5:]
    for b in range(out_ref.shape[0]):
        own, column, side = [refs[b][0] >> k & 1 == 1 for k in range(3)]

        @pl.when(own & column)
        def _():
            out_ref[b] = mine_ref[...]

        @pl.when(own & ~column)
        def _():
            out_ref[b] = came_ref[...]

        @pl.when(~own & side)
        def _():
            out_ref[b] = even_ref[b]

        @pl.when(~own & ~side)
        def _():
            out_ref[b] = odd_ref[b]


def step_on(words, mine, came, by_odd, by_even, cost):
    vmem = pl.BlockSpec(memory_space=pltpu.VMEM)
    return pl.pallas_call(
        step_kernel,
        out_shape=jax.ShapeDtypeStruct(by_odd.shape, by_odd.dtype),
        in_specs=[pl.BlockSpec(memory_space=pltpu.SMEM)] * len(words) + [vmem] * 4,
        out_specs=vmem,
        cost_estimate=cost,
        compiler_params=pltpu.CompilerParams(vmem_limit_bytes=VMEM),
        name="step_on",
    )(*words, mine, came, by_odd, by_even)


def flops(n):
    return pl.CostEstimate(flops=n, bytes_accessed=0, transcendentals=0)


def cost_of(step, q):
    return LONG if step < 4 or q == 1 else SHORT


def begin_kernel(*refs):
    mine_ref, came_ref, out_ref = refs[-3:]
    for b in range(out_ref.shape[0]):
        column = refs[b][0] >> 1 & 1 == 1

        @pl.when(column)
        def _():
            out_ref[b] = mine_ref[...]

        @pl.when(~column)
        def _():
            out_ref[b] = came_ref[...]


def begin(words, mine, came):
    vmem = pl.BlockSpec(memory_space=pltpu.VMEM)
    return pl.pallas_call(
        begin_kernel,
        out_shape=jax.ShapeDtypeStruct((len(words), *mine.shape), mine.dtype),
        in_specs=[pl.BlockSpec(memory_space=pltpu.SMEM)] * len(words) + [vmem] * 2,
        out_specs=vmem,
        cost_estimate=LONG,
        compiler_params=pltpu.CompilerParams(vmem_limit_bytes=VMEM),
        name="begin",
    )(*words, mine, came)


def choose_kernel(*refs):
    out_ref = refs[-1]
    batches = out_ref.shape[0]
    for b in range(batches):
        for k, ref in enumerate(refs[batches:-1]):

            @pl.when(refs[b][0] >> 3 == k)
            def _():
                out_ref[b] = ref[b]


def choose(words, window):
    vmem = pl.BlockSpec(memory_space=pltpu.VMEM)
    return pl.pallas_call(
        choose_kernel,
        out_shape=jax.ShapeDtypeStruct(window[0].shape, window[0].dtype),
        in_specs=[pl.BlockSpec(memory_space=pltpu.SMEM)] * len(words) + [vmem] * len(window),
        out_specs=vmem,
        cost_estimate=SHORT,
        compiler_params=pltpu.CompilerParams(vmem_limit_bytes=VMEM),
        name="choose",
    )(*words, *window)


def times_kernel(a_ref, w_ref, out_ref):
    out_ref[...] = jnp.dot(a_ref[...], w_ref[...], preferred_element_type=jnp.float32)


def times(a, w, aligned, cost):
    if not aligned:
        return jnp.dot(a, w, preferred_element_type=jnp.float32)
    vmem = pl.BlockSpec(memory_space=pltpu.VMEM)
    return pl.pallas_call(
        times_kernel,
        out_shape=jax.ShapeDtypeStruct((a.shape[0], w.shape[1]), jnp.float32),
        in_specs=[vmem, vmem],
        out_specs=vmem,
        cost_estimate=cost,
        compiler_params=pltpu.CompilerParams(vmem_limit_bytes=VMEM),
        name="times",
    )(a, w)


def settle_kernel(side_ref, here_ref, there_ref, keep_ref, coded_ref):
    side = side_ref[0]
    parts, _, rows, width = here_ref.shape
    lanes = LANES

    for o in range(width // lanes):
        at = slice(o * lanes, (o + 1) * lanes)
        give = []
        for p in range(parts):
            pair = [here_ref[p, k, :, at] + there_ref[p, k, :, at] for k in range(2)]
            keep_ref[p * rows : (p + 1) * rows, at] = jnp.where(side == 0, pair[0], pair[1])
            give.append(jnp.where(side == 0, pair[1], pair[0]))
        scaled, code = codes_of(jnp.concatenate(give, axis=0))
        coded_ref[: parts * rows, at] = scaled.astype(jnp.int32).astype(jnp.int16)
        coded_ref[parts * rows :, at] = jnp.broadcast_to(code, (TILE_ROWS, lanes)).astype(jnp.int32).astype(jnp.int16)


def settle(side, here, there):
    parts, _, rows, width = here.shape
    vmem = pl.BlockSpec(memory_space=pltpu.VMEM)
    return pl.pallas_call(
        settle_kernel,
        out_shape=(
            jax.ShapeDtypeStruct((parts * rows, width), jnp.float32),
            jax.ShapeDtypeStruct((parts * rows + TILE_ROWS, width), jnp.int16),
        ),
        in_specs=[pl.BlockSpec(memory_space=pltpu.SMEM), vmem, vmem],
        out_specs=(vmem, vmem),
        compiler_params=pltpu.CompilerParams(vmem_limit_bytes=VMEM),
        name="settle",
    )(side, here, there)


def merge_kernel(left_ref, keep_ref, coded_ref, total_ref, blocks_ref):
    left = left_ref[0] == 1
    _, rows, _ = keep_ref.shape
    parties, _, lanes = blocks_ref.shape

    for o in range(parties):
        at = slice(o * lanes, (o + 1) * lanes)
        step = step_of(coded_ref[2 * rows : 2 * rows + 1, at].astype(jnp.int32))
        first = keep_ref[0, :, at] + coded_ref[:rows, at].astype(jnp.float32) * step
        second = keep_ref[1, :, at] + coded_ref[rows : 2 * rows, at].astype(jnp.float32) * step
        total = jnp.concatenate([jnp.where(left, first, second), jnp.where(left, second, first)], axis=0)
        total_ref[:, at] = total
        scaled, code = codes_of(total)
        blocks_ref[o, : 2 * rows] = scaled.astype(jnp.int32).astype(jnp.int16)
        blocks_ref[o, 2 * rows :] = jnp.broadcast_to(code, (TILE_ROWS, lanes)).astype(jnp.int32).astype(jnp.int16)


def merge(left, left_word, keep, coded, parties, aligned):
    _, rows, width = keep.shape
    lanes = width // parties
    if not aligned:
        total = keep + grow(coded).reshape(keep.shape)
        total = jnp.where(left, total, total[::-1]).reshape(2 * rows, width)
        coded = shrink(total)
        return total, jnp.stack([coded[:, o * lanes : (o + 1) * lanes] for o in range(parties)])
    vmem = pl.BlockSpec(memory_space=pltpu.VMEM)
    return pl.pallas_call(
        merge_kernel,
        out_shape=(
            jax.ShapeDtypeStruct((2 * rows, width), jnp.float32),
            jax.ShapeDtypeStruct((parties, 2 * rows + TILE_ROWS, lanes), jnp.int16),
        ),
        in_specs=[pl.BlockSpec(memory_space=pltpu.SMEM), vmem, vmem],
        out_specs=(vmem, vmem),
        cost_estimate=SHORT,
        compiler_params=pltpu.CompilerParams(vmem_limit_bytes=VMEM),
        name="merge",
    )(left_word, keep, coded)


def finish_kernel(part, total_ref, blocks_ref, swap_ref, vir_ref, occ_ref, *rest):
    out_ref = rest[-1]
    batches, _, _, count, _ = out_ref.shape
    wide, padded, lanes = blocks_ref.shape
    rows = padded - TILE_ROWS
    half = occ_ref.shape[1] // 2
    swap = jnp.broadcast_to(swap_ref[...], (rows, lanes))
    occ = [jnp.transpose(jnp.broadcast_to(occ_ref[b : b + 1], (lanes, 2 * half))) for b in range(batches)]
    occ = [occ[b][h * half + part * count : h * half + (part + 1) * count] for h in range(2) for b in range(batches)]
    occ = jnp.concatenate(occ, axis=0)

    for o in range(wide):
        at = slice(o * lanes, (o + 1) * lanes)
        facing = blocks_ref[o, :rows].astype(jnp.float32) * step_of(blocks_ref[o, rows : rows + 1].astype(jnp.int32))
        both = total_ref[:, at] + jnp.take_along_axis(facing, swap, axis=1)
        both = both / (vir_ref[:, at] - occ)
        for h in range(2):
            for b in range(batches):
                first = (h * batches + b) * count
                out_ref[b, h, 0, :, at] = both[first : first + count]


def finish(total, blocks, swap_within, vir_energy, occ_energy, out, part, parts):
    rows, width = total.shape
    parties, padded, lanes = blocks.shape
    batches = occ_energy.shape[0]
    count = rows // 2 // batches
    wide = min(WIDE, parties)
    args = [total, blocks, swap_within.reshape(1, lanes), vir_energy.reshape(1, width), occ_energy]
    specs = [
        pl.BlockSpec((rows, wide * lanes), lambda i: (0, i)),
        pl.BlockSpec((wide, padded, lanes), lambda i: (i, 0, 0)),
        pl.BlockSpec((1, lanes), lambda i: (0, 0)),
        pl.BlockSpec((1, wide * lanes), lambda i: (0, i)),
        pl.BlockSpec(occ_energy.shape, lambda i: (0, 0)),
    ]
    alias = {}
    if out is not None:
        alias = {len(args): 0}
        args.append(out)
        specs.append(pl.BlockSpec(memory_space=pl.ANY))
    return pl.pallas_call(
        lambda *refs: finish_kernel(part, *refs),
        grid=(parties // wide,),
        out_shape=jax.ShapeDtypeStruct((batches, 2, parts, count, width), jnp.float32),
        in_specs=specs,
        out_specs=pl.BlockSpec((batches, 2, 1, count, wide * lanes), lambda i: (0, 0, part, 0, i)),
        input_output_aliases=alias,
        cost_estimate=LONG,
        compiler_params=pltpu.CompilerParams(vmem_limit_bytes=VMEM),
        name="finish",
    )(*args)


def on_device(integrals, amplitudes, tile_live, batch_owner, occ_energy, vir_energy, swap_within):
    parties, groups = lax.axis_size("outpair"), lax.axis_size("inpair")
    nz, bits = parties // 2, groups.bit_length() - 1
    batches = batch_owner.shape[0]
    _, rows, depth = amplitudes.shape
    width = integrals.shape[1]
    lanes = width // parties
    share = rows // groups
    half = share // 2
    streams, chunks = (STREAMS, CHUNKS) if half % (16 * STREAMS * CHUNKS) == 0 else (1, 1)
    parts = chunks
    deep = half // (streams * chunks)
    aligned = lanes % LANES == 0 and share % LANES == 0 and bits == 2
    beside = [(o, o ^ 1) for o in range(parties)]
    even = [(o, o ^ 2) for o in range(parties) if (o ^ 2) < parties]
    odd = [(o, ((o // 2 + 1) ^ 1) * 2 - 2 + o % 2) for o in range(parties)]
    odd = [(o, t) for o, t in odd if 0 <= t < parties]

    def swap_x(values):
        return lax.ppermute(values, "outpair", beside)

    def shift(values):
        return lax.ppermute(values, "outpair", odd), lax.ppermute(values, "outpair", even)

    def cut(a, q, c):
        return a[:, (c * streams + q) * deep : (c * streams + q + 1) * deep]

    me, place = lax.axis_index("outpair").astype(jnp.uint32), lax.axis_index("inpair").astype(jnp.uint32)
    x, z = me & 1, me >> 1
    stored = amplitudes[0].reshape(groups, 2, half, depth)
    other = pick(stored, 1 - x, 1)
    zero = jnp.uint32(0)
    first = lax.dynamic_slice(stored, (zero, 1 - x, zero, zero), (groups, 1, deep, depth))[:, 0]
    came = [[swap_x(first)]]
    other = pick(tied(stored, first), 1 - x, 1)
    came[0] += [swap_x(tied(cut(other, q, 0), came[0][0])) for q in range(1, streams)]
    came += [swap_x(tied(jnp.stack([cut(other, q, c) for q in range(streams)]), came[0][0])) for c in range(1, chunks)]

    owner = [batch_owner[b].astype(jnp.uint32) for b in range(batches)]
    scalars = dict(
        x=x,
        left=x == 0,
        own=[z == o >> 1 for o in owner],
        mine=[x == o & 1 for o in owner],
        from_even=[(z > o >> 1) == (z & 1 == 1) for o in owner],
        far=[jnp.where(z > o >> 1, z - (o >> 1), (o >> 1) - z) for o in owner],
        side=[place >> k & 1 for k in range(bits)],
        not_side=[1 - (place >> k & 1) for k in range(bits)],
        words=[
            (
                (z == o >> 1).astype(jnp.int32)
                + 2 * (x == o & 1).astype(jnp.int32)
                + 4 * ((z > o >> 1) == (z & 1 == 1)).astype(jnp.int32)
                + 8 * jnp.where(z > o >> 1, z - (o >> 1), (o >> 1) - z).astype(jnp.int32)
            ).reshape(1)
            for o in owner
        ],
        left_word=(x == 0).astype(jnp.int32).reshape(1),
        side_word=(place >> 1 & 1).astype(jnp.int32).reshape(1),
    )
    tall_tile, wide_tile = integrals.shape[0] // tile_live.shape[0], width // tile_live.shape[1]
    flags = jnp.repeat(tile_live.astype(jnp.bfloat16), wide_tile, 1)[:, None, :]
    live = (integrals.reshape(-1, tall_tile, width) * flags).reshape(integrals.shape)
    mine = pick(stored, x, 1)
    came[0][0], mine, scalars = lax.optimization_barrier((came[0][0], mine, scalars))
    left, own, from_even, distance = scalars["left"], scalars["own"], scalars["from_even"], scalars["far"]
    side, not_side = scalars["side"], scalars["not_side"]

    keeps, sent, coded = {}, {}, {}

    def sum_part(p, n, f):
        tall = jnp.stack([jnp.concatenate(n, axis=2), jnp.concatenate(f, axis=2)])
        count = tall.shape[3]
        tall = tall.reshape(2 * batches, groups // 2, 2, count, depth)
        away = pick(tall, not_side[0], 2).reshape(-1, depth)
        stay = pick(tall, side[0], 2).reshape(-1, depth)
        there = lax.ppermute(times(away, live, aligned, LONG if p else SHORT), "inpair", [(g, g ^ 1) for g in range(groups)])
        here = times(stay, live, aligned, LONG if p else SHORT)
        across = lambda k: [(g, g ^ (1 << k)) for g in range(groups)]
        if aligned:
            shape = (2 * batches, 2, count, width)
            keep, sent[p] = settle(scalars["side_word"], here.reshape(shape), there.reshape(shape))
            coded[p] = lax.ppermute(sent[p], "inpair", across(1))
        else:
            total = (here + there).reshape(2 * batches, groups // 2, count, width)
            for k in range(1, bits):
                split = total.reshape(2 * batches, total.shape[1] // 2, 2, count, width)
                keep, give = pick(split, side[k], 2), pick(split, not_side[k], 2)
                sent[p] = shrink(give.reshape(-1, width))
                coded[p] = lax.ppermute(sent[p], "inpair", across(k))
                if k + 1 < bits:
                    total = keep + grow(coded[p]).reshape(keep.shape)
        keeps[p] = keep.reshape(2, batches * count, width)
        return sent[p]

    def advance(q, c, by_odd, by_even, cost):
        if aligned:
            return step_on(scalars["words"], cut(mine, q, c), came[c][q], by_odd, by_even, cost)
        own_chunk = [jnp.where(m, cut(mine, q, c), came[c][q]) for m in scalars["mine"]]
        return jnp.stack(
            [jnp.where(own[b], own_chunk[b], jnp.where(from_even[b], by_even[b], by_odd[b])) for b in range(batches)]
        )

    def settled(window):
        if aligned:
            return choose(scalars["words"], window)
        return jnp.stack([pick(jnp.stack([h[b] for h in window]), distance[b], 0) for b in range(batches)])

    held = []
    near, far = [[] for _ in range(streams)], [[] for _ in range(streams)]
    for q in range(streams):
        if aligned:
            start = begin(scalars["words"], cut(mine, q, 0), came[0][q])
        else:
            start = jnp.stack([jnp.where(m, cut(mine, q, 0), came[0][q]) for m in scalars["mine"]])
        held.append([start])
    moved = [shift(h[0]) for h in held]
    for step in range(1, chunks + nz - 1):
        for q in range(streams):
            arrived = moved[q]
            held[q].append(advance(q, min(step, chunks - 1), *arrived, cost_of(step, q)))
            if step < chunks + nz - 2:
                moved[q] = shift(held[q][-1])
            if step >= nz - 1:
                near[q].append(settled(held[q][step - nz + 1 : step + 1]))
                far[q].append(swap_x(near[q][-1]))

    word = scalars["left_word"]
    merged = {}
    for p in range(parts):
        n, f = [near[q][p] for q in range(streams)], [far[q][p] for q in range(streams)]
        if p:
            n, f = tied((n, f), *[sent[k] for k in range(p)])
        sum_part(p, n, f)
    for p in range(parts):
        back = tied(coded[p], *[sent[k] for k in range(p + 1, parts)])
        merged[p] = merge(left, word, keeps[p], back, parties, aligned)
    order = range(parts)

    out, parted = None, []
    for p in order:
        total, blocks = merged[p]
        blocks = lax.all_to_all(blocks, "outpair", split_axis=0, concat_axis=0, tiled=True)
        if aligned:
            out = finish(total, blocks, swap_within, vir_energy, occ_energy, out, p, parts)
            continue
        facing = jnp.concatenate([jnp.take(grow(blocks[o]), swap_within, axis=1) for o in range(parties)], axis=1)
        parted.append((total + facing).reshape(2, batches, -1, width))
    if aligned:
        return out.reshape(batches, share, width)
    whole = jnp.transpose(jnp.concatenate(parted, axis=2), (1, 0, 2, 3)).reshape(batches, share, width)
    return whole / (vir_energy[None, None, :] - occ_energy[:, :, None])


def solution(mesh):
    return jax.shard_map(
        on_device,
        mesh=mesh,
        in_specs=(
            P("inpair", "outpair"),
            P("outpair", None, "inpair"),
            P("inpair", "outpair"),
            P(),
            P(None, "inpair"),
            P("outpair"),
            P(),
        ),
        out_specs=P(None, "inpair", "outpair"),
        check_vma=False,
    )
```

```python
import jax
import jax.numpy as jnp
from jax import lax
from jax.experimental import pallas as pl
from jax.experimental.pallas import tpu as pltpu
from jax.sharding import PartitionSpec as P

CHUNKS = 2
STREAMS = 2
LEVELS = 32767.0
OCTAVE = 128.0
LANES = 128
TILE_ROWS = 16
WIDE = 8
VMEM = 8 * 1024 * 1024
SHORT = pl.CostEstimate(flops=1_000_000, bytes_accessed=0, transcendentals=0)
LONG = pl.CostEstimate(flops=20_000_000_000, bytes_accessed=0, transcendentals=0)


def pick(array, index, axis):
    return lax.dynamic_index_in_dim(array, index, axis, keepdims=False)


def tied(values, *others):
    return lax.optimization_barrier((values, *others))[0]


def codes_of(values):
    top = jnp.max(jnp.abs(values), axis=0, keepdims=True)
    code = jnp.ceil(jnp.log2(jnp.maximum(top, 1e-30)) * OCTAVE)
    scaled = jnp.round(values * (LEVELS * jnp.exp2(code * (-1.0 / OCTAVE))))
    return jnp.clip(scaled, -LEVELS, LEVELS), code


def step_of(code):
    return jnp.exp2(code.astype(jnp.float32) * (1.0 / OCTAVE)) * (1.0 / LEVELS)


def shrink(values):
    scaled, code = codes_of(values)
    return jnp.concatenate([scaled.astype(jnp.int16), code.astype(jnp.int16)], axis=0)


def grow(coded):
    return coded[:-1].astype(jnp.float32) * step_of(coded[-1:])


def step_kernel(*refs):
    mine_ref, came_ref, odd_ref, even_ref, out_ref = refs[-5:]
    for b in range(out_ref.shape[0]):
        own, column, side = [refs[b][0] >> k & 1 == 1 for k in range(3)]

        @pl.when(own & column)
        def _():
            out_ref[b] = mine_ref[...]

        @pl.when(own & ~column)
        def _():
            out_ref[b] = came_ref[...]

        @pl.when(~own & side)
        def _():
            out_ref[b] = even_ref[b]

        @pl.when(~own & ~side)
        def _():
            out_ref[b] = odd_ref[b]


def step_on(words, mine, came, by_odd, by_even, cost):
    vmem = pl.BlockSpec(memory_space=pltpu.VMEM)
    return pl.pallas_call(
        step_kernel,
        out_shape=jax.ShapeDtypeStruct(by_odd.shape, by_odd.dtype),
        in_specs=[pl.BlockSpec(memory_space=pltpu.SMEM)] * len(words) + [vmem] * 4,
        out_specs=vmem,
        cost_estimate=cost,
        compiler_params=pltpu.CompilerParams(vmem_limit_bytes=VMEM),
        name="step_on",
    )(*words, mine, came, by_odd, by_even)


def flops(n):
    return pl.CostEstimate(flops=n, bytes_accessed=0, transcendentals=0)


def cost_of(step, q):
    return LONG if step < 4 or q == 1 else SHORT


def begin_kernel(*refs):
    mine_ref, came_ref, out_ref = refs[-3:]
    for b in range(out_ref.shape[0]):
        column = refs[b][0] >> 1 & 1 == 1

        @pl.when(column)
        def _():
            out_ref[b] = mine_ref[...]

        @pl.when(~column)
        def _():
            out_ref[b] = came_ref[...]


def begin(words, mine, came):
    vmem = pl.BlockSpec(memory_space=pltpu.VMEM)
    return pl.pallas_call(
        begin_kernel,
        out_shape=jax.ShapeDtypeStruct((len(words), *mine.shape), mine.dtype),
        in_specs=[pl.BlockSpec(memory_space=pltpu.SMEM)] * len(words) + [vmem] * 2,
        out_specs=vmem,
        cost_estimate=LONG,
        compiler_params=pltpu.CompilerParams(vmem_limit_bytes=VMEM),
        name="begin",
    )(*words, mine, came)


def choose_kernel(*refs):
    out_ref = refs[-1]
    batches = out_ref.shape[0]
    for b in range(batches):
        for k, ref in enumerate(refs[batches:-1]):

            @pl.when(refs[b][0] >> 3 == k)
            def _():
                out_ref[b] = ref[b]


def choose(words, window):
    vmem = pl.BlockSpec(memory_space=pltpu.VMEM)
    return pl.pallas_call(
        choose_kernel,
        out_shape=jax.ShapeDtypeStruct(window[0].shape, window[0].dtype),
        in_specs=[pl.BlockSpec(memory_space=pltpu.SMEM)] * len(words) + [vmem] * len(window),
        out_specs=vmem,
        cost_estimate=SHORT,
        compiler_params=pltpu.CompilerParams(vmem_limit_bytes=VMEM),
        name="choose",
    )(*words, *window)


def times_kernel(a_ref, w_ref, out_ref):
    out_ref[...] = jnp.dot(a_ref[...], w_ref[...], preferred_element_type=jnp.float32)


def times(a, w, aligned, cost):
    if not aligned:
        return jnp.dot(a, w, preferred_element_type=jnp.float32)
    vmem = pl.BlockSpec(memory_space=pltpu.VMEM)
    return pl.pallas_call(
        times_kernel,
        out_shape=jax.ShapeDtypeStruct((a.shape[0], w.shape[1]), jnp.float32),
        in_specs=[vmem, vmem],
        out_specs=vmem,
        cost_estimate=cost,
        compiler_params=pltpu.CompilerParams(vmem_limit_bytes=VMEM),
        name="times",
    )(a, w)


def settle_kernel(side_ref, here_ref, there_ref, keep_ref, coded_ref):
    side = side_ref[0]
    parts, _, rows, width = here_ref.shape
    lanes = LANES

    for o in range(width // lanes):
        at = slice(o * lanes, (o + 1) * lanes)
        give = []
        for p in range(parts):
            pair = [here_ref[p, k, :, at] + there_ref[p, k, :, at] for k in range(2)]
            keep_ref[p * rows : (p + 1) * rows, at] = jnp.where(side == 0, pair[0], pair[1])
            give.append(jnp.where(side == 0, pair[1], pair[0]))
        scaled, code = codes_of(jnp.concatenate(give, axis=0))
        coded_ref[: parts * rows, at] = scaled.astype(jnp.int32).astype(jnp.int16)
        coded_ref[parts * rows :, at] = jnp.broadcast_to(code, (TILE_ROWS, lanes)).astype(jnp.int32).astype(jnp.int16)


def settle(side, here, there):
    parts, _, rows, width = here.shape
    vmem = pl.BlockSpec(memory_space=pltpu.VMEM)
    return pl.pallas_call(
        settle_kernel,
        out_shape=(
            jax.ShapeDtypeStruct((parts * rows, width), jnp.float32),
            jax.ShapeDtypeStruct((parts * rows + TILE_ROWS, width), jnp.int16),
        ),
        in_specs=[pl.BlockSpec(memory_space=pltpu.SMEM), vmem, vmem],
        out_specs=(vmem, vmem),
        compiler_params=pltpu.CompilerParams(vmem_limit_bytes=VMEM),
        name="settle",
    )(side, here, there)


def merge_kernel(left_ref, keep_ref, coded_ref, total_ref, blocks_ref):
    left = left_ref[0] == 1
    _, rows, _ = keep_ref.shape
    parties, _, lanes = blocks_ref.shape

    for o in range(parties):
        at = slice(o * lanes, (o + 1) * lanes)
        step = step_of(coded_ref[2 * rows : 2 * rows + 1, at].astype(jnp.int32))
        first = keep_ref[0, :, at] + coded_ref[:rows, at].astype(jnp.float32) * step
        second = keep_ref[1, :, at] + coded_ref[rows : 2 * rows, at].astype(jnp.float32) * step
        total = jnp.concatenate([jnp.where(left, first, second), jnp.where(left, second, first)], axis=0)
        total_ref[:, at] = total
        scaled, code = codes_of(total)
        blocks_ref[o, : 2 * rows] = scaled.astype(jnp.int32).astype(jnp.int16)
        blocks_ref[o, 2 * rows :] = jnp.broadcast_to(code, (TILE_ROWS, lanes)).astype(jnp.int32).astype(jnp.int16)


def merge(left, left_word, keep, coded, parties, aligned):
    _, rows, width = keep.shape
    lanes = width // parties
    if not aligned:
        total = keep + grow(coded).reshape(keep.shape)
        total = jnp.where(left, total, total[::-1]).reshape(2 * rows, width)
        coded = shrink(total)
        return total, jnp.stack([coded[:, o * lanes : (o + 1) * lanes] for o in range(parties)])
    vmem = pl.BlockSpec(memory_space=pltpu.VMEM)
    return pl.pallas_call(
        merge_kernel,
        out_shape=(
            jax.ShapeDtypeStruct((2 * rows, width), jnp.float32),
            jax.ShapeDtypeStruct((parties, 2 * rows + TILE_ROWS, lanes), jnp.int16),
        ),
        in_specs=[pl.BlockSpec(memory_space=pltpu.SMEM), vmem, vmem],
        out_specs=(vmem, vmem),
        cost_estimate=SHORT,
        compiler_params=pltpu.CompilerParams(vmem_limit_bytes=VMEM),
        name="merge",
    )(left_word, keep, coded)


def finish_kernel(part, total_ref, blocks_ref, swap_ref, vir_ref, occ_ref, *rest):
    out_ref = rest[-1]
    batches, _, _, count, _ = out_ref.shape
    wide, padded, lanes = blocks_ref.shape
    rows = padded - TILE_ROWS
    half = occ_ref.shape[1] // 2
    swap = jnp.broadcast_to(swap_ref[...], (rows, lanes))
    occ = [jnp.transpose(jnp.broadcast_to(occ_ref[b : b + 1], (lanes, 2 * half))) for b in range(batches)]
    occ = [occ[b][h * half + part * count : h * half + (part + 1) * count] for h in range(2) for b in range(batches)]
    occ = jnp.concatenate(occ, axis=0)

    for o in range(wide):
        at = slice(o * lanes, (o + 1) * lanes)
        facing = blocks_ref[o, :rows].astype(jnp.float32) * step_of(blocks_ref[o, rows : rows + 1].astype(jnp.int32))
        both = total_ref[:, at] + jnp.take_along_axis(facing, swap, axis=1)
        both = both / (vir_ref[:, at] - occ)
        for h in range(2):
            for b in range(batches):
                first = (h * batches + b) * count
                out_ref[b, h, 0, :, at] = both[first : first + count]


def finish(total, blocks, swap_within, vir_energy, occ_energy, out, part, parts):
    rows, width = total.shape
    parties, padded, lanes = blocks.shape
    batches = occ_energy.shape[0]
    count = rows // 2 // batches
    wide = min(WIDE, parties)
    args = [total, blocks, swap_within.reshape(1, lanes), vir_energy.reshape(1, width), occ_energy]
    specs = [
        pl.BlockSpec((rows, wide * lanes), lambda i: (0, i)),
        pl.BlockSpec((wide, padded, lanes), lambda i: (i, 0, 0)),
        pl.BlockSpec((1, lanes), lambda i: (0, 0)),
        pl.BlockSpec((1, wide * lanes), lambda i: (0, i)),
        pl.BlockSpec(occ_energy.shape, lambda i: (0, 0)),
    ]
    alias = {}
    if out is not None:
        alias = {len(args): 0}
        args.append(out)
        specs.append(pl.BlockSpec(memory_space=pl.ANY))
    return pl.pallas_call(
        lambda *refs: finish_kernel(part, *refs),
        grid=(parties // wide,),
        out_shape=jax.ShapeDtypeStruct((batches, 2, parts, count, width), jnp.float32),
        in_specs=specs,
        out_specs=pl.BlockSpec((batches, 2, 1, count, wide * lanes), lambda i: (0, 0, part, 0, i)),
        input_output_aliases=alias,
        cost_estimate=LONG,
        compiler_params=pltpu.CompilerParams(vmem_limit_bytes=VMEM),
        name="finish",
    )(*args)


def on_device(integrals, amplitudes, tile_live, batch_owner, occ_energy, vir_energy, swap_within):
    parties, groups = lax.axis_size("outpair"), lax.axis_size("inpair")
    nz, bits = parties // 2, groups.bit_length() - 1
    batches = batch_owner.shape[0]
    _, rows, depth = amplitudes.shape
    width = integrals.shape[1]
    lanes = width // parties
    share = rows // groups
    half = share // 2
    streams, chunks = (STREAMS, CHUNKS) if half % (16 * STREAMS * CHUNKS) == 0 else (1, 1)
    parts = chunks
    deep = half // (streams * chunks)
    aligned = lanes % LANES == 0 and share % LANES == 0 and bits == 2
    beside = [(o, o ^ 1) for o in range(parties)]
    even = [(o, o ^ 2) for o in range(parties) if (o ^ 2) < parties]
    odd = [(o, ((o // 2 + 1) ^ 1) * 2 - 2 + o % 2) for o in range(parties)]
    odd = [(o, t) for o, t in odd if 0 <= t < parties]

    def swap_x(values):
        return lax.ppermute(values, "outpair", beside)

    def shift(values):
        return lax.ppermute(values, "outpair", odd), lax.ppermute(values, "outpair", even)

    def cut(a, q, c):
        return a[:, (c * streams + q) * deep : (c * streams + q + 1) * deep]

    me, place = lax.axis_index("outpair").astype(jnp.uint32), lax.axis_index("inpair").astype(jnp.uint32)
    x, z = me & 1, me >> 1
    stored = amplitudes[0].reshape(groups, 2, half, depth)
    other = pick(stored, 1 - x, 1)
    zero = jnp.uint32(0)
    first = lax.dynamic_slice(stored, (zero, 1 - x, zero, zero), (groups, 1, deep, depth))[:, 0]
    came = [[swap_x(first)]]
    other = pick(tied(stored, first), 1 - x, 1)
    came[0] += [swap_x(tied(cut(other, q, 0), came[0][0])) for q in range(1, streams)]
    came += [swap_x(tied(jnp.stack([cut(other, q, c) for q in range(streams)]), came[0][0])) for c in range(1, chunks)]

    owner = [batch_owner[b].astype(jnp.uint32) for b in range(batches)]
    scalars = dict(
        x=x,
        left=x == 0,
        own=[z == o >> 1 for o in owner],
        mine=[x == o & 1 for o in owner],
        from_even=[(z > o >> 1) == (z & 1 == 1) for o in owner],
        far=[jnp.where(z > o >> 1, z - (o >> 1), (o >> 1) - z) for o in owner],
        side=[place >> k & 1 for k in range(bits)],
        not_side=[1 - (place >> k & 1) for k in range(bits)],
        words=[
            (
                (z == o >> 1).astype(jnp.int32)
                + 2 * (x == o & 1).astype(jnp.int32)
                + 4 * ((z > o >> 1) == (z & 1 == 1)).astype(jnp.int32)
                + 8 * jnp.where(z > o >> 1, z - (o >> 1), (o >> 1) - z).astype(jnp.int32)
            ).reshape(1)
            for o in owner
        ],
        left_word=(x == 0).astype(jnp.int32).reshape(1),
        side_word=(place >> 1 & 1).astype(jnp.int32).reshape(1),
    )
    tall_tile, wide_tile = integrals.shape[0] // tile_live.shape[0], width // tile_live.shape[1]
    flags = jnp.repeat(tile_live.astype(jnp.bfloat16), wide_tile, 1)[:, None, :]
    live = (integrals.reshape(-1, tall_tile, width) * flags).reshape(integrals.shape)
    mine = pick(stored, x, 1)
    came[0][0], mine, scalars = lax.optimization_barrier((came[0][0], mine, scalars))
    left, own, from_even, distance = scalars["left"], scalars["own"], scalars["from_even"], scalars["far"]
    side, not_side = scalars["side"], scalars["not_side"]

    keeps, sent, coded = {}, {}, {}

    def sum_part(p, n, f):
        tall = jnp.stack([jnp.concatenate(n, axis=2), jnp.concatenate(f, axis=2)])
        count = tall.shape[3]
        tall = tall.reshape(2 * batches, groups // 2, 2, count, depth)
        away = pick(tall, not_side[0], 2).reshape(-1, depth)
        stay = pick(tall, side[0], 2).reshape(-1, depth)
        there = lax.ppermute(times(away, live, aligned, LONG if p else SHORT), "inpair", [(g, g ^ 1) for g in range(groups)])
        here = times(stay, live, aligned, LONG if p else SHORT)
        across = lambda k: [(g, g ^ (1 << k)) for g in range(groups)]
        if aligned:
            shape = (2 * batches, 2, count, width)
            keep, sent[p] = settle(scalars["side_word"], here.reshape(shape), there.reshape(shape))
            coded[p] = lax.ppermute(sent[p], "inpair", across(1))
        else:
            total = (here + there).reshape(2 * batches, groups // 2, count, width)
            for k in range(1, bits):
                split = total.reshape(2 * batches, total.shape[1] // 2, 2, count, width)
                keep, give = pick(split, side[k], 2), pick(split, not_side[k], 2)
                sent[p] = shrink(give.reshape(-1, width))
                coded[p] = lax.ppermute(sent[p], "inpair", across(k))
                if k + 1 < bits:
                    total = keep + grow(coded[p]).reshape(keep.shape)
        keeps[p] = keep.reshape(2, batches * count, width)
        return sent[p]

    def advance(q, c, by_odd, by_even, cost):
        if aligned:
            return step_on(scalars["words"], cut(mine, q, c), came[c][q], by_odd, by_even, cost)
        own_chunk = [jnp.where(m, cut(mine, q, c), came[c][q]) for m in scalars["mine"]]
        return jnp.stack(
            [jnp.where(own[b], own_chunk[b], jnp.where(from_even[b], by_even[b], by_odd[b])) for b in range(batches)]
        )

    def settled(window):
        if aligned:
            return choose(scalars["words"], window)
        return jnp.stack([pick(jnp.stack([h[b] for h in window]), distance[b], 0) for b in range(batches)])

    held = []
    near, far = [[] for _ in range(streams)], [[] for _ in range(streams)]
    for q in range(streams):
        if aligned:
            start = begin(scalars["words"], cut(mine, q, 0), came[0][q])
        else:
            start = jnp.stack([jnp.where(m, cut(mine, q, 0), came[0][q]) for m in scalars["mine"]])
        held.append([start])
    moved = [shift(h[0]) for h in held]
    for step in range(1, chunks + nz - 1):
        for q in range(streams):
            arrived = moved[q]
            held[q].append(advance(q, min(step, chunks - 1), *arrived, cost_of(step, q)))
            if step < chunks + nz - 2:
                moved[q] = shift(held[q][-1])
            if step >= nz - 1:
                near[q].append(settled(held[q][step - nz + 1 : step + 1]))
                far[q].append(swap_x(near[q][-1]))

    word = scalars["left_word"]
    merged = {}
    for p in range(parts):
        n, f = [near[q][p] for q in range(streams)], [far[q][p] for q in range(streams)]
        if p:
            n, f = tied((n, f), *[sent[k] for k in range(p)])
        sum_part(p, n, f)
    for p in range(parts):
        back = tied(coded[p], *[sent[k] for k in range(p + 1, parts)])
        merged[p] = merge(left, word, keeps[p], back, parties, aligned)
    order = range(parts)

    out, parted = None, []
    for p in order:
        total, blocks = merged[p]
        blocks = lax.all_to_all(blocks, "outpair", split_axis=0, concat_axis=0, tiled=True)
        if aligned:
            out = finish(total, blocks, swap_within, vir_energy, occ_energy, out, p, parts)
            continue
        facing = jnp.concatenate([jnp.take(grow(blocks[o]), swap_within, axis=1) for o in range(parties)], axis=1)
        parted.append((total + facing).reshape(2, batches, -1, width))
    if aligned:
        return out.reshape(batches, share, width)
    whole = jnp.transpose(jnp.concatenate(parted, axis=2), (1, 0, 2, 3)).reshape(batches, share, width)
    return whole / (vir_energy[None, None, :] - occ_energy[:, :, None])


def solution(mesh):
    return jax.shard_map(
        on_device,
        mesh=mesh,
        in_specs=(
            P("inpair", "outpair"),
            P("outpair", None, "inpair"),
            P("inpair", "outpair"),
            P(),
            P(None, "inpair"),
            P("outpair"),
            P(),
        ),
        out_specs=P(None, "inpair", "outpair"),
        check_vma=False,
    )
```
